256 devices in a mesh: fsdp: 64 (over y, z, core), rep: 4 (over x).
Axes of the slice: x: 4, y: 4, z: 8, core: 2. Of those that a mesh axis runs over, the one named last changes fastest.
Arguments:
- grads: bfloat16 [4, 2, 4096, 8192], P('rep', None, 'fsdp'), may hold values from -0.375 to 0.375
- slot_block: int32 [64], replicated, may hold values from 0 to 63, each once
- left_gram: float32 [64, 1024, 1024], P('fsdp', 'rep'), may hold values from -1 to 40, as said below
- right_gram: float32 [64, 1024, 1024], P('fsdp', 'rep'), may hold values from -1 to 40, as said below
- left_root: bfloat16 [64, 1024, 1024], P('fsdp', 'rep'), may hold values from -0.061 to 4, as said below
- right_root: bfloat16 [64, 1024, 1024], P('fsdp', None, 'rep'), may hold values from -0.061 to 4, as said below
Outputs:
- new_left: float32 [64, 1024, 1024], P('fsdp', 'rep')
- new_right: float32 [64, 1024, 1024], P('fsdp', 'rep')
- update: bfloat16 [2, 4096, 8192], P(None, ('fsdp', 'rep'))
The draws below stay inside these ranges and needn't reach their ends.
Inputs may be any that keep to these rules, and one draw needn't show every extreme that they name: `slot_block`: a permutation of the 64 blocks; slot k lies on fsdp index k. `left_gram`: symmetric in the last two dimensions. `right_gram`: symmetric in the last two dimensions. `left_root`: symmetric in the last two dimensions. `right_root`: symmetric in the last two dimensions.
All inputs are finite; a program needn't handle non-finite values.
Results may differ from the reference program's by a relative error of at most 0.015.
Values may be sent and summed in bfloat16 or wider, within the bound.
A program may use at most 128 MiB of HBM per device.

```python
import math
import jax
import jax.numpy as jnp
from jax import lax

D = 8192
BS = 1024
RW = 4096
NB = 64
N_REP = 4


def symmetric_matrix(key, entries, lowest, highest, clip_value):
    order_size = entries.shape[-1]
    row_ids = lax.broadcasted_iota(jnp.int32, (order_size, order_size), 0)
    col_ids = lax.broadcasted_iota(jnp.int32, (order_size, order_size), 1)
    spread = jnp.exp(jax.random.uniform(key, entries.shape[:-1], jnp.float32, math.log(lowest), math.log(highest)))
    off_diagonal = jnp.clip(entries + jnp.swapaxes(entries, -1, -2), -clip_value, clip_value)
    return jnp.where(row_ids == col_ids, spread[..., None], off_diagonal)


def draw_left_gram(key, part):
    key = jax.random.fold_in(key, 11)
    key_one, key_two = jax.random.split(key)
    entries = 0.25 * jax.random.truncated_normal(key_one, -2.0, 2.0, (NB, BS, BS), jnp.float32)
    return symmetric_matrix(key_two, entries, 4.0, 40.0, 1.0)


def draw_right_gram(key, part):
    key = jax.random.fold_in(key, 17)
    key_one, key_two = jax.random.split(key)
    entries = 0.25 * jax.random.truncated_normal(key_one, -2.0, 2.0, (NB, BS, BS), jnp.float32)
    return symmetric_matrix(key_two, entries, 4.0, 40.0, 1.0)


def draw_left_root(key, part):
    key = jax.random.fold_in(key, 23)
    key_one, key_two = jax.random.split(key)
    limit_value = 0.9 / math.sqrt(BS)
    entries = 0.5 * limit_value * jax.random.truncated_normal(key_one, -2.0, 2.0, (NB, BS, BS), jnp.float32)
    return symmetric_matrix(key_two, entries, 1.5, 4.0, 0.06).astype(jnp.bfloat16)


def draw_right_root(key, part):
    key = jax.random.fold_in(key, 29)
    key_one, key_two = jax.random.split(key)
    limit_value = 0.9 / math.sqrt(BS)
    entries = 0.5 * limit_value * jax.random.truncated_normal(key_one, -2.0, 2.0, (NB, BS, BS), jnp.float32)
    return symmetric_matrix(key_two, entries, 1.5, 4.0, 0.06).astype(jnp.bfloat16)


def shard_levels(stream_key, shape, cuts, least, top_value):
    loudness, own = 1.0, jax.random.fold_in(stream_key, 6)
    for dim, blocks in cuts:
        draws = jnp.exp(jax.random.uniform(jax.random.fold_in(own, dim), (blocks,), jnp.float32, least / len(cuts), top_value / len(cuts)))
        loudness = loudness * jnp.repeat(draws, shape[dim] // blocks).reshape([-1 if axis == dim else 1 for axis in range(len(shape))])
    return loudness


def centred(stream_key, dims, deviation, most, cuts=(), kind=jnp.bfloat16):
    values = deviation * jax.random.normal(stream_key, dims, jnp.float32)
    if cuts:
        values = values * shard_levels(stream_key, dims, cuts, -0.22, 0.18)
    return jnp.clip(values, -most, most).astype(kind)


def setup_inputs(seed: int = 0) -> dict:
    splits = jax.random.split(jax.random.key(seed), 7)
    return {
        "grads": centred(splits[0], (N_REP, 2, RW, D), 0.0625, 0.375, ((0, 4), (2, 64))),
        "slot_block": jax.random.permutation(splits[1], NB).astype(jnp.int32),
        "left_gram": draw_left_gram(jax.random.fold_in(splits[6], 71), 0),
        "right_gram": draw_right_gram(jax.random.fold_in(splits[6], 71), 0),
        "left_root": draw_left_root(jax.random.fold_in(splits[6], 71), 0),
        "right_root": draw_right_root(jax.random.fold_in(splits[6], 71), 0),
    }


def reference(grads, slot_block, left_gram, right_gram, left_root, right_root):
    row_blocks = RW // BS
    col_blocks = D // BS
    summed = jnp.sum(grads, axis=0, dtype=jnp.float32).astype(jnp.bfloat16)
    blocks = summed.reshape(2, row_blocks, BS, col_blocks, BS).transpose(0, 1, 3, 2, 4).reshape(NB, BS, BS)

    def one_slot(operands):
        block_id, left_old, right_old, left_inv, right_inv = operands
        gradient = blocks[block_id]
        new_left = left_old + jnp.dot(gradient, gradient.T, preferred_element_type=jnp.float32)
        new_right = right_old + jnp.dot(gradient.T, gradient, preferred_element_type=jnp.float32)
        right_mixed = jnp.dot(gradient, right_inv, preferred_element_type=jnp.float32).astype(jnp.bfloat16)
        preconditioned = jnp.dot(left_inv, right_mixed, preferred_element_type=jnp.float32).astype(jnp.bfloat16)
        return new_left, new_right, preconditioned

    new_left, new_right, preconditioned = lax.map(one_slot, (slot_block, left_gram, right_gram, left_root, right_root))
    slot_of = jnp.zeros((NB,), jnp.int32).at[slot_block].set(jnp.arange(NB, dtype=jnp.int32))
    by_block = preconditioned[slot_of]
    update = by_block.reshape(2, row_blocks, col_blocks, BS, BS).transpose(0, 1, 3, 2, 4).reshape(2, RW, D)
    return new_left, new_right, update
```

```python
import functools

import jax
import jax.numpy as jnp
from jax import lax
from jax.experimental import pallas as pl
from jax.experimental.pallas import tpu as pltpu
from jax.sharding import PartitionSpec as P

MESH = pl.DeviceIdType.MESH
BF16 = jnp.bfloat16
F32 = jnp.float32
N_LOCAL, N_SEND, N_RECV = 20, 64, 64


def dot(a, b, dims):
    return lax.dot_general(a, b, (dims, ((), ())), preferred_element_type=F32)


def kernel(
    sizes,
    slot_block, slot_place, grads, left_gram, right_gram, left_root, right_root,
    new_left, new_right, update,
    gv, rs1, psend, rs2, ysum, yrecv0, yrecv1, tsend, trecv, g, l2, r2, nbuf, pbuf, pa, pb,
    csend, cr, lg, rg, upd, lsem, ssem, rsem,
):
    ny, nt, jb, cw = sizes
    mj = 2 * jb
    bs = 8 * cw
    half = nt // 2
    per = nt // 4
    units = 4 // ny
    rr = bs // nt // 4
    yrecv = (yrecv0, yrecv1)
    s = lax.axis_index("fsdp")
    x = lax.axis_index("rep")
    y = lax.div(s, nt)
    t = lax.rem(s, nt)
    xa = x + 1 - 2 * lax.rem(x, 2)
    xb = 3 - x
    xo = lax.rem(x + 2, 4)
    xhalf = lax.div(x, 2)
    pair = jnp.minimum(x, xb)
    y_steps = (ny // 2, *[d for d in range(1, ny) if d != ny // 2])

    counters = {"l": 0, "s": 0, "r": 0}

    def take(kind):
        counters[kind] += 1
        return counters[kind] - 1

    sends = []
    own = {}

    def dev(xx, yy, tt):
        return (yy * nt + tt, xx)

    def remote(src, dst, si, ri, to):
        pltpu.make_async_remote_copy(
            src_ref=src, dst_ref=dst, send_sem=ssem.at[si], recv_sem=rsem.at[ri],
            device_id=to, device_id_type=MESH,
        ).start()

    def local(src, dst):
        copy = pltpu.make_async_copy(src, dst, lsem.at[take("l")])
        copy.start()
        return copy

    def await_recv(ref, ri):
        pltpu.make_async_copy(ref, ref, rsem.at[ri]).wait()

    copy_gv = local(grads, gv)
    copy_l = local(left_root.at[0], l2.at[lax.rem(x, 2)])
    copy_r = local(right_root.at[0], r2.at[xhalf])
    copy_lg = local(left_gram.at[0], lg)
    copy_rg = local(right_gram.at[0], rg)

    barrier = pltpu.get_barrier_semaphore()
    for dx in range(4):
        for dy in range(ny):
            if dx or dy:
                to = dev(lax.rem(x + dx, 4), lax.rem(y + dy, ny), t)
                pl.semaphore_signal(barrier, inc=1, device_id=to, device_id_type=MESH)

    def greet(d, carry):
        to = dev(x, y, lax.rem(t + d, nt))
        pl.semaphore_signal(barrier, inc=1, device_id=to, device_id_type=MESH)
        return carry

    lax.fori_loop(1, nt, greet, 0)
    pl.semaphore_wait(barrier, 4 * ny - 1 + nt - 1)

    def cols(j, q, c):
        return pl.ds(pl.multiple_of(j * bs + q * 2 * cw + c * cw, cw), cw)

    rs1_r = [[[take("r") for _ in range(2)] for _ in range(2)] for _ in range(2)]
    rs2_r = [[take("r") for _ in range(2)] for _ in range(2)]

    def rs1_start(c):
        for w in (1, 0):
            si = [take("s") for _ in range(2)]

            def one(j, carry, w=w, si=si):
                for m, to_x in enumerate((xa, xb)):
                    q = xo if w == 1 else to_x
                    remote(
                        grads.at[m, :, :, cols(j, q, c)], rs1.at[c, m, w, j],
                        si[m], rs1_r[c][m][w], dev(to_x, y, t),
                    )
                return carry

            lax.fori_loop(0, jb, one, 0)
            for m in range(2):
                sends.append((rs1.at[c, m, w], si[m]))

    def rs2_start(c):
        for m, to_x in enumerate((xb, xa)):
            await_recv(rs1.at[c, m, 1], rs1_r[c][m][1])

            def one(j, carry, m=m, to_x=to_x):
                mine = gv[m, :, :, cols(j, to_x, c)].astype(F32)
                psend[c, m, j] = (mine + rs1[c, m, 1, j].astype(F32)).astype(BF16)
                return carry

            lax.fori_loop(0, jb, one, 0)
            si = take("s")
            remote(psend.at[c, m], rs2.at[c, m], si, rs2_r[c][m], dev(to_x, y, t))
            sends.append((psend.at[c, m], si))

    y1_r = [take("r") for _ in range(2)]
    t_r = [take("r") for _ in range(2)]
    y2_r = [take("r") for _ in range(2)]

    def y1_start(c):
        for m in range(2):
            await_recv(rs1.at[c, m, 0], rs1_r[c][m][0])
            await_recv(rs2.at[c, m], rs2_r[c][m])

            def one(j, carry, m=m):
                mine = gv[m, :, :, cols(j, x, c)].astype(F32)
                total = mine + rs1[c, m, 0, j].astype(F32) + rs2[c, m, j].astype(F32)
                ysum[c, :, m * jb + j] = total.astype(BF16)
                return carry

            lax.fori_loop(0, jb, one, 0)
        si = take("s")
        place = pl.ds(y * mj, mj)
        for d in y_steps:
            yy = lax.rem(y + d, ny)
            remote(ysum.at[c, yy], yrecv[c].at[place], si, y1_r[c], dev(x, yy, t))
        sends.append((ysum.at[c, pl.ds(0, ny - 1)], si))
        own["y1", c] = local(ysum.at[c, y], yrecv[c].at[place])

    def t_start(c):
        await_recv(yrecv[c].at[pl.ds(0, (ny - 1) * mj)], y1_r[c])
        own["y1", c].wait()
        si = take("s")

        def pick(tt):
            for yy in range(ny):
                b = slot_block[yy * nt + tt]
                row = lax.rem(lax.div(b, jb), ny)
                m = lax.div(b, jb * ny)
                tsend[c, tt, yy] = yrecv[c][row * mj + m * jb + lax.rem(b, jb)]

        def one(d, carry):
            tt = lax.rem(t + d, nt)
            pick(tt)
            remote(tsend.at[c, tt], trecv.at[c, t], si, t_r[c], dev(x, y, tt))
            return carry

        lax.fori_loop(1, nt, one, 0)
        pick(t)
        sends.append((tsend.at[c, pl.ds(0, nt - 1)], si))
        own["t", c] = local(tsend.at[c, t], trecv.at[c, t])

    def gcols(c):
        return pl.ds(c * cw, cw)

    def y2_start(c):
        await_recv(trecv.at[c, pl.ds(0, nt - 1)], t_r[c])
        own["t", c].wait()
        si = take("s")
        place = g.at[x, :, y, :, gcols(c)]
        for d in y_steps:
            yy = lax.rem(y + d, ny)
            remote(trecv.at[c, :, yy], place, si, y2_r[c], dev(x, yy, t))
        sends.append((trecv.at[c, :, pl.ds(0, ny - 1)], si))
        own["y2", c] = local(trecv.at[c, :, y], place)

    ag1_r = [[[take("r") for _ in range(2)] for _ in range(2)] for _ in range(2)]
    ag2_r = [[take("r") for _ in range(2)] for _ in range(2)]

    def gpart(q, h, c):
        return g.at[q, pl.ds(h * half, half), :, :, gcols(c)]

    def ag1_start(c):
        await_recv(g.at[x, :, pl.ds(0, ny - 1), :, gcols(c)], y2_r[c])
        own["y2", c].wait()
        for first in (True, False):
            for e, to_x in enumerate((xa, xb)):
                h = e if first else 1 - e
                part = gpart(x, h, c)
                si = take("s")
                remote(part, part, si, ag1_r[c][e][h], dev(to_x, y, t))
                sends.append((part, si))

    def ag2_start(c):
        for e, (source, to_x) in enumerate(((xa, xb), (xb, xa))):
            part = gpart(source, e, c)
            await_recv(part, ag1_r[c][e][e])
            si = take("s")
            remote(part, part, si, ag2_r[c][e], dev(to_x, y, t))
            sends.append((part, si))

    rs1_start(0)
    copy_gv.wait()
    rs2_start(0)
    rs1_start(1)
    y1_start(0)
    rs2_start(1)
    l_s, r_s, l_r, r_r = take("s"), take("s"), take("r"), take("r")
    remote(left_root.at[0], l2.at[lax.rem(x, 2)], l_s, l_r, dev(xa, y, t))
    remote(right_root.at[0], r2.at[xhalf], r_s, r_r, dev(xb, y, t))
    sends.append((l2.at[0], l_s))
    sends.append((r2.at[0], r_s))
    t_start(0)
    y1_start(1)
    y2_start(0)
    t_start(1)
    ag1_start(0)
    ag2_start(0)
    y2_start(1)
    ag1_start(1)
    ag2_start(1)

    def block_cols(q):
        return g[q].reshape(bs, 2 * cw)

    def rows_times(q):
        part = dot(l2[...].reshape(bs // 2, bs), block_cols(q), ((1,), (0,)))
        nbuf[:, pl.ds(pl.multiple_of(q * 2 * cw, 2 * cw), 2 * cw)] = part.astype(BF16)

    copy_l.wait()
    await_recv(l2.at[0], l_r)
    rows_times(x)
    for e, source in enumerate((xa, xb)):
        await_recv(gpart(source, 1 - e, 0), ag1_r[0][e][1 - e])
        await_recv(gpart(source, 1 - e, 1), ag1_r[1][e][1 - e])
        rows_times(source)
    for c in range(2):
        for e in range(2):
            await_recv(gpart(xo, e, c), ag2_r[c][e])
    rows_times(xo)

    copy_r.wait()
    await_recv(r2.at[0], r_r)
    for w in range(2):
        part = dot(nbuf[...], r2[w], ((1,), (0,))).astype(BF16)
        for h in range(2):
            pbuf[2 * w + h] = part[:, h * cw : (h + 1) * cw].reshape(half, 4, rr, cw)

    a_s = [take("s") for _ in range(4)]
    a_r = [take("r") for _ in range(4)]
    a_place = pa.at[y, :, pair, pl.ds(xhalf * half, half)]
    for dx in (2, 1, 3, 0):
        for dy in range(ny):
            xx, yy = lax.rem(x + dx, 4), lax.rem(y + dy, ny)
            src = pbuf.at[pl.ds(yy * units, units), :, xx]
            if dx or dy:
                remote(src, a_place, a_s[dx], a_r[dx], dev(xx, yy, t))
            else:
                own["a"] = local(src, a_place)

    def a_bytes(dx):
        return pa.at[pl.ds(0, ny if dx else ny - 1), :, 0, pl.ds(0, half)]

    for dx in range(4):
        sends.append((a_bytes(dx), a_s[dx]))

    copy_lg.wait()
    for q in range(4):
        rows = g[q, pl.ds(x * per, per)].reshape(bs // 4, 2 * cw)
        lg[...] += dot(rows, block_cols(q), ((1,), (1,)))
    out_left = local(lg, new_left.at[0])

    for dx in range(4):
        await_recv(a_bytes(dx), a_r[dx])
    own["a"].wait()
    b_s, b_r = take("s"), take("r")
    b_place = pb.at[pl.ds(t * ny, ny)]

    def stripe(d, carry):
        tt = lax.rem(t + d, nt)
        remote(pa.at[:, :, :, tt], b_place, b_s, b_r, dev(x, y, tt))
        return carry

    lax.fori_loop(1, nt, stripe, 0)
    own["b"] = local(pa.at[:, :, :, t], b_place)
    sends.append((pb.at[pl.ds(0, (nt - 1) * ny)], b_s))

    copy_rg.wait()
    turned = block_cols(x).T
    for q in range(4):
        part = pl.ds(q * 2 * cw, 2 * cw)
        rg[:, part] += dot(turned, block_cols(q), ((1,), (0,)))
    out_right = local(rg, new_right.at[0])

    await_recv(pb.at[pl.ds(0, (nt - 1) * ny)], b_r)
    own["b"].wait()

    def collect(yy):
        def one(j, carry):
            for m in range(2):
                csend[yy, m * jb + j] = pb[slot_place[(m * ny + yy) * jb + j]]
            return carry

        lax.fori_loop(0, jb, one, 0)

    c_s = [take("s") for _ in range(ny)]
    c_r = [take("r") for _ in range(ny)]
    for d in y_steps:
        yy = lax.rem(y + d, ny)
        collect(yy)
        remote(csend.at[yy], cr.at[y], c_s[d], c_r[d], dev(x, yy, t))
        sends.append((csend.at[0], c_s[d]))
    collect(y)

    def lay(src, slab, yy):
        for u in range(units):
            unit = yy * units + u
            w, h = lax.div(unit, 2), lax.rem(unit, 2)
            for p in range(2):
                quarter = p + w * (3 - 2 * p)

                def one(j, carry, u=u, h=h, p=p, quarter=quarter):
                    for m in range(2):
                        at = pl.multiple_of(j * bs + quarter * 2 * cw + h * cw, cw)
                        upd[m, :, pl.ds(at, cw)] = src[slab, m * jb + j, u, p]
                    return carry

                lax.fori_loop(0, jb, one, 0)

    lay(csend, y, y)
    for d in y_steps:
        yy = lax.rem(y - d + ny, ny)
        await_recv(cr.at[yy], c_r[d])
        lay(cr, yy, yy)
    out_update = local(upd, update)

    for ref, si in sends:
        pltpu.make_async_copy(ref, ref, ssem.at[si]).wait()
    out_left.wait()
    out_right.wait()
    out_update.wait()
    assert counters["l"] <= N_LOCAL and counters["s"] <= N_SEND and counters["r"] <= N_RECV


def body(ny, grads, slot_block, left_gram, right_gram, left_root, right_root):
    owners = lax.axis_size("fsdp")
    nt = owners // ny
    bs = left_gram.shape[2]
    stripe, width = grads.shape[2], grads.shape[3]
    jb = width // bs
    mj = 2 * jb
    cw = bs // 8
    sr = stripe // ny
    rr = stripe // 4
    units = 4 // ny
    ids = jnp.arange(owners, dtype=jnp.int32)
    place = (ids % nt) * ny + ids // nt
    slot_place = jnp.sum(
        jnp.where(slot_block[None, :] == ids[:, None], place[None, :], 0), axis=1
    )
    vm = pltpu.VMEM
    scratch = [
        vm((2, ny, sr, width), BF16),
        vm((2, 2, 2, jb, ny, sr, cw), BF16),
        vm((2, 2, jb, ny, sr, cw), BF16),
        vm((2, 2, jb, ny, sr, cw), BF16),
        vm((2, ny, mj, sr, cw), BF16),
        vm((ny * mj, sr, cw), BF16),
        vm((ny * mj, sr, cw), BF16),
        vm((2, nt, ny, sr, cw), BF16),
        vm((2, nt, ny, sr, cw), BF16),
        vm((4, nt, ny, sr, 2 * cw), BF16),
        vm((2, bs // 4, bs), BF16),
        vm((2, bs, 2 * cw), BF16),
        vm((bs // 2, bs), BF16),
        vm((4, nt // 2, 4, rr, cw), BF16),
        vm((ny, units, 2, nt, rr, cw), BF16),
        vm((nt * ny, units, 2, rr, cw), BF16),
        vm((ny, mj, units, 2, rr, cw), BF16),
        vm((ny, mj, units, 2, rr, cw), BF16),
        vm((bs // 4, bs), F32),
        vm((bs // 4, bs), F32),
        vm((2, rr, width), BF16),
        pltpu.SemaphoreType.DMA((N_LOCAL,)),
        pltpu.SemaphoreType.DMA((N_SEND,)),
        pltpu.SemaphoreType.DMA((N_RECV,)),
    ]
    whole = pl.BlockSpec(memory_space=pl.ANY)
    table = pl.BlockSpec(memory_space=pltpu.SMEM)
    return pl.pallas_call(
        functools.partial(kernel, (ny, nt, jb, cw)),
        out_shape=(
            jax.ShapeDtypeStruct(left_gram.shape, F32),
            jax.ShapeDtypeStruct(right_gram.shape, F32),
            jax.ShapeDtypeStruct((2, rr, width), BF16),
        ),
        in_specs=[table, table, whole, whole, whole, whole, whole],
        out_specs=(whole, whole, whole),
        scratch_shapes=scratch,
        compiler_params=pltpu.CompilerParams(
            collective_id=0, has_side_effects=True, vmem_limit_bytes=48 * 1024 * 1024
        ),
        cost_estimate=pl.CostEstimate(
            flops=5 * bs**3 // 2, bytes_accessed=12 * bs * bs, transcendentals=0
        ),
        name="shampoo",
    )(
        slot_block, slot_place, grads.reshape(2, ny, sr, width),
        left_gram, right_gram, left_root, right_root,
    )


def solution(mesh, ny=4):
    in_specs = (
        P("rep", None, "fsdp", None),
        P(),
        P("fsdp", "rep", None),
        P("fsdp", "rep", None),
        P("fsdp", "rep", None),
        P("fsdp", None, "rep"),
    )
    out_specs = (P("fsdp", "rep", None), P("fsdp", "rep", None), P(None, ("fsdp", "rep"), None))
    return jax.shard_map(
        functools.partial(body, ny), mesh=mesh, in_specs=in_specs, out_specs=out_specs,
        check_vma=False,
    )
```

```python
import functools

import jax
import jax.numpy as jnp
from jax import lax
from jax.experimental import pallas as pl
from jax.experimental.pallas import tpu as pltpu
from jax.sharding import PartitionSpec as P

MESH = pl.DeviceIdType.MESH
BF16 = jnp.bfloat16
F32 = jnp.float32
N_LOCAL, N_SEND, N_RECV = 20, 64, 64


def dot(a, b, dims):
    return lax.dot_general(a, b, (dims, ((), ())), preferred_element_type=F32)


def kernel(
    sizes,
    slot_block, grads, left_gram, right_gram, left_root, right_root,
    lg, rg, upd,
    gv, rs1, psend, rs2, ysum, yrecv0, yrecv1, tsend, trecv, g, l2, r2, nbuf, pbuf, pa, pb,
    csend, cr, place_row, slot_table, slot_place, lsem, ssem, rsem,
):
    ny, nt, jb, cw = sizes
    mj = 2 * jb
    bs = 8 * cw
    half = nt // 2
    per = nt // 4
    units = 4 // ny
    rr = bs // nt // 4
    yrecv = (yrecv0, yrecv1)
    s = lax.axis_index("fsdp")
    x = lax.axis_index("rep")
    y = lax.div(s, nt)
    t = lax.rem(s, nt)
    xa = x + 1 - 2 * lax.rem(x, 2)
    xb = 3 - x
    xo = lax.rem(x + 2, 4)
    xhalf = lax.div(x, 2)
    pair = jnp.minimum(x, xb)
    y_steps = (ny // 2, *[d for d in range(1, ny) if d != ny // 2])

    counters = {"l": 0, "s": 0, "r": 0}

    def take(kind):
        counters[kind] += 1
        return counters[kind] - 1

    sends = []
    own = {}

    def dev(xx, yy, tt):
        return (yy * nt + tt, xx)

    def remote(src, dst, si, ri, to):
        pltpu.make_async_remote_copy(
            src_ref=src, dst_ref=dst, send_sem=ssem.at[si], recv_sem=rsem.at[ri],
            device_id=to, device_id_type=MESH,
        ).start()

    def local(src, dst):
        copy = pltpu.make_async_copy(src, dst, lsem.at[take("l")])
        copy.start()
        return copy

    def await_recv(ref, ri):
        pltpu.make_async_copy(ref, ref, rsem.at[ri]).wait()

    copy_table = local(slot_block, slot_table)
    copy_gv = local(grads, gv)
    copy_l = local(left_root.at[0], l2.at[lax.rem(x, 2)])
    copy_r = local(right_root.at[0], r2.at[xhalf])
    copy_lg = local(left_gram, lg)
    copy_rg = local(right_gram, rg)

    copy_table.wait()
    lanes = lax.broadcasted_iota(jnp.int32, place_row.shape, 1)

    def turn(k, row):
        at = lax.rem(k, nt) * ny + lax.div(k, nt)
        return jnp.where(lanes == slot_table[k], at, row)

    place_row[...] = lax.fori_loop(0, ny * nt, turn, jnp.zeros_like(lanes))
    copy_place = local(place_row, slot_place)

    barrier = pltpu.get_barrier_semaphore()
    for dx in range(4):
        for dy in range(ny):
            if dx or dy:
                to = dev(lax.rem(x + dx, 4), lax.rem(y + dy, ny), t)
                pl.semaphore_signal(barrier, inc=1, device_id=to, device_id_type=MESH)

    def greet(d, carry):
        to = dev(x, y, lax.rem(t + d, nt))
        pl.semaphore_signal(barrier, inc=1, device_id=to, device_id_type=MESH)
        return carry

    lax.fori_loop(1, nt, greet, 0)
    pl.semaphore_wait(barrier, 4 * ny - 1 + nt - 1)

    def cols(j, q, c):
        return pl.ds(pl.multiple_of(j * bs + q * 2 * cw + c * cw, cw), cw)

    rs1_r = [[[take("r") for _ in range(2)] for _ in range(2)] for _ in range(2)]
    rs2_r = [[take("r") for _ in range(2)] for _ in range(2)]

    def rs1_start(c):
        for w in (1, 0):
            si = [take("s") for _ in range(2)]

            def one(j, carry, w=w, si=si):
                for m, to_x in enumerate((xa, xb)):
                    q = xo if w == 1 else to_x
                    remote(
                        grads.at[m, :, :, cols(j, q, c)], rs1.at[c, m, w, j],
                        si[m], rs1_r[c][m][w], dev(to_x, y, t),
                    )
                return carry

            lax.fori_loop(0, jb, one, 0)
            for m in range(2):
                sends.append((rs1.at[c, m, w], si[m]))

    def rs2_start(c):
        for m, to_x in enumerate((xb, xa)):
            await_recv(rs1.at[c, m, 1], rs1_r[c][m][1])

            def one(j, carry, m=m, to_x=to_x):
                mine = gv[m, :, :, cols(j, to_x, c)].astype(F32)
                psend[c, m, j] = (mine + rs1[c, m, 1, j].astype(F32)).astype(BF16)
                return carry

            lax.fori_loop(0, jb, one, 0)
            si = take("s")
            remote(psend.at[c, m], rs2.at[c, m], si, rs2_r[c][m], dev(to_x, y, t))
            sends.append((psend.at[c, m], si))

    y1_r = [take("r") for _ in range(2)]
    t_r = [take("r") for _ in range(2)]
    y2_r = [take("r") for _ in range(2)]

    def y1_start(c):
        for m in range(2):
            await_recv(rs1.at[c, m, 0], rs1_r[c][m][0])
            await_recv(rs2.at[c, m], rs2_r[c][m])

            def one(j, carry, m=m):
                mine = gv[m, :, :, cols(j, x, c)].astype(F32)
                total = mine + rs1[c, m, 0, j].astype(F32) + rs2[c, m, j].astype(F32)
                ysum[c, :, m * jb + j] = total.astype(BF16)
                return carry

            lax.fori_loop(0, jb, one, 0)
        si = take("s")
        place = pl.ds(y * mj, mj)
        for d in y_steps:
            yy = lax.rem(y + d, ny)
            remote(ysum.at[c, yy], yrecv[c].at[place], si, y1_r[c], dev(x, yy, t))
        sends.append((ysum.at[c, pl.ds(0, ny - 1)], si))
        own["y1", c] = local(ysum.at[c, y], yrecv[c].at[place])

    def t_start(c):
        await_recv(yrecv[c].at[pl.ds(0, (ny - 1) * mj)], y1_r[c])
        own["y1", c].wait()
        si = take("s")

        def pick(tt):
            for yy in range(ny):
                b = slot_table[yy * nt + tt]
                row = lax.rem(lax.div(b, jb), ny)
                m = lax.div(b, jb * ny)
                tsend[c, tt, yy] = yrecv[c][row * mj + m * jb + lax.rem(b, jb)]

        def one(d, carry):
            tt = lax.rem(t + d, nt)
            pick(tt)
            remote(tsend.at[c, tt], trecv.at[c, t], si, t_r[c], dev(x, y, tt))
            return carry

        lax.fori_loop(1, nt, one, 0)
        pick(t)
        sends.append((tsend.at[c, pl.ds(0, nt - 1)], si))
        own["t", c] = local(tsend.at[c, t], trecv.at[c, t])

    def gcols(c):
        return pl.ds(c * cw, cw)

    def y2_start(c):
        await_recv(trecv.at[c, pl.ds(0, nt - 1)], t_r[c])
        own["t", c].wait()
        si = take("s")
        place = g.at[x, :, y, :, gcols(c)]
        for d in y_steps:
            yy = lax.rem(y + d, ny)
            remote(trecv.at[c, :, yy], place, si, y2_r[c], dev(x, yy, t))
        sends.append((trecv.at[c, :, pl.ds(0, ny - 1)], si))
        own["y2", c] = local(trecv.at[c, :, y], place)

    ag1_r = [[[take("r") for _ in range(2)] for _ in range(2)] for _ in range(2)]
    ag2_r = [[take("r") for _ in range(2)] for _ in range(2)]

    def gpart(q, h, c):
        return g.at[q, pl.ds(h * half, half), :, :, gcols(c)]

    def ag1_start(c):
        await_recv(g.at[x, :, pl.ds(0, ny - 1), :, gcols(c)], y2_r[c])
        own["y2", c].wait()
        for first in (True, False):
            for e, to_x in enumerate((xa, xb)):
                h = e if first else 1 - e
                part = gpart(x, h, c)
                si = take("s")
                remote(part, part, si, ag1_r[c][e][h], dev(to_x, y, t))
                sends.append((part, si))

    def ag2_start(c):
        for e, (source, to_x) in enumerate(((xa, xb), (xb, xa))):
            part = gpart(source, e, c)
            await_recv(part, ag1_r[c][e][e])
            si = take("s")
            remote(part, part, si, ag2_r[c][e], dev(to_x, y, t))
            sends.append((part, si))

    rs1_start(0)
    copy_gv.wait()
    rs2_start(0)
    rs1_start(1)
    y1_start(0)
    rs2_start(1)
    l_s, r_s, l_r, r_r = take("s"), take("s"), take("r"), take("r")
    remote(left_root.at[0], l2.at[lax.rem(x, 2)], l_s, l_r, dev(xa, y, t))
    remote(right_root.at[0], r2.at[xhalf], r_s, r_r, dev(xb, y, t))
    sends.append((l2.at[0], l_s))
    sends.append((r2.at[0], r_s))
    t_start(0)
    y1_start(1)
    y2_start(0)
    t_start(1)
    ag1_start(0)
    ag2_start(0)
    y2_start(1)
    ag1_start(1)
    ag2_start(1)

    def block_cols(q):
        return g[q].reshape(bs, 2 * cw)

    def rows_times(q):
        part = dot(l2[...].reshape(bs // 2, bs), block_cols(q), ((1,), (0,)))
        nbuf[:, pl.ds(pl.multiple_of(q * 2 * cw, 2 * cw), 2 * cw)] = part.astype(BF16)

    copy_l.wait()
    await_recv(l2.at[0], l_r)
    rows_times(x)
    for e, source in enumerate((xa, xb)):
        await_recv(gpart(source, 1 - e, 0), ag1_r[0][e][1 - e])
        await_recv(gpart(source, 1 - e, 1), ag1_r[1][e][1 - e])
        rows_times(source)
    for c in range(2):
        for e in range(2):
            await_recv(gpart(xo, e, c), ag2_r[c][e])
    rows_times(xo)

    copy_r.wait()
    await_recv(r2.at[0], r_r)
    for w in range(2):
        part = dot(nbuf[...], r2[w], ((1,), (0,))).astype(BF16)
        for h in range(2):
            pbuf[2 * w + h] = part[:, h * cw : (h + 1) * cw].reshape(half, 4, rr, cw)

    a_s = [take("s") for _ in range(4)]
    a_r = [take("r") for _ in range(4)]
    a_place = pa.at[y, :, pair, pl.ds(xhalf * half, half)]
    for dx in (2, 1, 3, 0):
        for dy in range(ny):
            xx, yy = lax.rem(x + dx, 4), lax.rem(y + dy, ny)
            src = pbuf.at[pl.ds(yy * units, units), :, xx]
            if dx or dy:
                remote(src, a_place, a_s[dx], a_r[dx], dev(xx, yy, t))
            else:
                own["a"] = local(src, a_place)

    def a_bytes(dx):
        return pa.at[pl.ds(0, ny if dx else ny - 1), :, 0, pl.ds(0, half)]

    for dx in range(4):
        sends.append((a_bytes(dx), a_s[dx]))

    copy_lg.wait()
    for q in range(4):
        rows = g[q, pl.ds(x * per, per)].reshape(bs // 4, 2 * cw)
        lg[0] += dot(rows, block_cols(q), ((1,), (1,)))

    for dx in range(4):
        await_recv(a_bytes(dx), a_r[dx])
    own["a"].wait()
    b_s, b_r = take("s"), take("r")
    b_place = pb.at[pl.ds(t * ny, ny)]

    def stripe(d, carry):
        tt = lax.rem(t + d, nt)
        remote(pa.at[:, :, :, tt], b_place, b_s, b_r, dev(x, y, tt))
        return carry

    lax.fori_loop(1, nt, stripe, 0)
    own["b"] = local(pa.at[:, :, :, t], b_place)
    sends.append((pb.at[pl.ds(0, (nt - 1) * ny)], b_s))

    copy_rg.wait()
    turned = block_cols(x).T
    for q in range(4):
        part = pl.ds(q * 2 * cw, 2 * cw)
        rg[0, :, part] += dot(turned, block_cols(q), ((1,), (0,)))

    await_recv(pb.at[pl.ds(0, (nt - 1) * ny)], b_r)
    own["b"].wait()
    copy_place.wait()

    def collect(yy):
        def one(j, carry):
            for m in range(2):
                csend[yy, m * jb + j] = pb[slot_place[0, (m * ny + yy) * jb + j]]
            return carry

        lax.fori_loop(0, jb, one, 0)

    c_s = [take("s") for _ in range(ny)]
    c_r = [take("r") for _ in range(ny)]
    for d in y_steps:
        yy = lax.rem(y + d, ny)
        collect(yy)
        remote(csend.at[yy], cr.at[y], c_s[d], c_r[d], dev(x, yy, t))
        sends.append((csend.at[0], c_s[d]))
    collect(y)

    def lay(src, slab, yy):
        for u in range(units):
            unit = yy * units + u
            w, h = lax.div(unit, 2), lax.rem(unit, 2)
            for p in range(2):
                quarter = p + w * (3 - 2 * p)

                def one(j, carry, u=u, h=h, p=p, quarter=quarter):
                    for m in range(2):
                        at = pl.multiple_of(j * bs + quarter * 2 * cw + h * cw, cw)
                        upd[m, :, pl.ds(at, cw)] = src[slab, m * jb + j, u, p]
                    return carry

                lax.fori_loop(0, jb, one, 0)

    lay(csend, y, y)
    for d in y_steps:
        yy = lax.rem(y - d + ny, ny)
        await_recv(cr.at[yy], c_r[d])
        lay(cr, yy, yy)

    for ref, si in sends:
        pltpu.make_async_copy(ref, ref, ssem.at[si]).wait()
    assert counters["l"] <= N_LOCAL and counters["s"] <= N_SEND and counters["r"] <= N_RECV


def hand_on(*refs):
    sem = refs[-1]
    copies = [pltpu.make_async_copy(refs[i], refs[3 + i], sem.at[i]) for i in range(3)]
    for copy in copies:
        copy.start()
    for copy in copies:
        copy.wait()


def body(ny, grads, slot_block, left_gram, right_gram, left_root, right_root):
    owners = lax.axis_size("fsdp")
    nt = owners // ny
    bs = left_gram.shape[2]
    stripe, width = grads.shape[2], grads.shape[3]
    jb = width // bs
    mj = 2 * jb
    cw = bs // 8
    sr = stripe // ny
    rr = stripe // 4
    units = 4 // ny
    vm = pltpu.VMEM
    scratch = [
        vm((2, ny, sr, width), BF16),
        vm((2, 2, 2, jb, ny, sr, cw), BF16),
        vm((2, 2, jb, ny, sr, cw), BF16),
        vm((2, 2, jb, ny, sr, cw), BF16),
        vm((2, ny, mj, sr, cw), BF16),
        vm((ny * mj, sr, cw), BF16),
        vm((ny * mj, sr, cw), BF16),
        vm((2, nt, ny, sr, cw), BF16),
        vm((2, nt, ny, sr, cw), BF16),
        vm((4, nt, ny, sr, 2 * cw), BF16),
        vm((2, bs // 4, bs), BF16),
        vm((2, bs, 2 * cw), BF16),
        vm((bs // 2, bs), BF16),
        vm((4, nt // 2, 4, rr, cw), BF16),
        vm((ny, units, 2, nt, rr, cw), BF16),
        vm((nt * ny, units, 2, rr, cw), BF16),
        vm((ny, mj, units, 2, rr, cw), BF16),
        vm((ny, mj, units, 2, rr, cw), BF16),
        vm((1, 128), jnp.int32),
        pltpu.SMEM((ny * nt,), jnp.int32),
        pltpu.SMEM((1, 128), jnp.int32),
        pltpu.SemaphoreType.DMA((N_LOCAL,)),
        pltpu.SemaphoreType.DMA((N_SEND,)),
        pltpu.SemaphoreType.DMA((N_RECV,)),
    ]
    whole = pl.BlockSpec(memory_space=pltpu.HBM)
    inside = pl.BlockSpec(memory_space=pltpu.VMEM)
    operands = (
        slot_block, grads.reshape(2, ny, sr, width), left_gram, right_gram, left_root, right_root
    )
    outs = pl.pallas_call(
        functools.partial(kernel, (ny, nt, jb, cw)),
        out_shape=(
            pltpu.VMEM(left_gram.shape, F32),
            pltpu.VMEM(right_gram.shape, F32),
            pltpu.VMEM((2, rr, width), BF16),
        ),
        in_specs=[whole, whole, whole, whole, whole, whole],
        out_specs=(inside,) * 3,
        scratch_shapes=scratch,
        compiler_params=pltpu.CompilerParams(
            collective_id=0, has_side_effects=True, vmem_limit_bytes=48 * 1024 * 1024
        ),
        cost_estimate=pl.CostEstimate(
            flops=5 * bs**3 // 2, bytes_accessed=12 * bs * bs, transcendentals=0
        ),
        name="shampoo",
    )(
        *(pltpu.with_memory_space_constraint(a, pltpu.HBM) for a in operands)
    )
    return pl.pallas_call(
        hand_on,
        out_shape=tuple(pltpu.HBM(a.shape, a.dtype) for a in outs),
        in_specs=[inside] * 3,
        out_specs=(whole,) * 3,
        scratch_shapes=[pltpu.SemaphoreType.DMA((3,))],
        name="hand_on",
    )(*(pltpu.with_memory_space_constraint(a, pltpu.VMEM) for a in outs))


def solution(mesh, ny=4):
    in_specs = (
        P("rep", None, "fsdp", None),
        P(),
        P("fsdp", "rep", None),
        P("fsdp", "rep", None),
        P("fsdp", "rep", None),
        P("fsdp", None, "rep"),
    )
    out_specs = (P("fsdp", "rep", None), P("fsdp", "rep", None), P(None, ("fsdp", "rep"), None))
    return jax.shard_map(
        functools.partial(body, ny), mesh=mesh, in_specs=in_specs, out_specs=out_specs,
        check_vma=False,
    )
```

```python
import functools

import jax
import jax.numpy as jnp
from jax import lax
from jax.experimental import pallas as pl
from jax.experimental.pallas import tpu as pltpu
from jax.sharding import PartitionSpec as P

MESH = pl.DeviceIdType.MESH
BF16 = jnp.bfloat16
F32 = jnp.float32
N_LOCAL, N_SEND, N_RECV = 20, 64, 64


def dot(a, b, dims):
    return lax.dot_general(a, b, (dims, ((), ())), preferred_element_type=F32)


def kernel(
    sizes,
    slot_block, grads, left_gram, right_gram, left_root, right_root,
    lg, rg, upd,
    gv, rs1, psend, rs2, ysum, yrecv0, yrecv1, tsend, trecv, g, l2, r2, nbuf, pbuf, pa, pb,
    csend, cr, place_row, slot_table, slot_place, lsem, ssem, rsem,
):
    ny, nt, jb, cw = sizes
    mj = 2 * jb
    bs = 8 * cw
    half = nt // 2
    per = nt // 4
    rr = bs // nt // 4
    yrecv = (yrecv0, yrecv1)
    s = lax.axis_index("fsdp")
    x = lax.axis_index("rep")
    y = lax.div(s, nt)
    t = lax.rem(s, nt)
    xa = x + 1 - 2 * lax.rem(x, 2)
    xb = 3 - x
    xo = lax.rem(x + 2, 4)
    xhalf = lax.div(x, 2)
    pair = jnp.minimum(x, xb)
    y_steps = (ny // 2, *[d for d in range(1, ny) if d != ny // 2])

    counters = {"l": 0, "s": 0, "r": 0}

    def take(kind):
        counters[kind] += 1
        return counters[kind] - 1

    sends = []
    own = {}

    def dev(xx, yy, tt):
        return (yy * nt + tt, xx)

    def remote(src, dst, si, ri, to):
        pltpu.make_async_remote_copy(
            src_ref=src, dst_ref=dst, send_sem=ssem.at[si], recv_sem=rsem.at[ri],
            device_id=to, device_id_type=MESH,
        ).start()

    def local(src, dst):
        copy = pltpu.make_async_copy(src, dst, lsem.at[take("l")])
        copy.start()
        return copy

    def await_recv(ref, ri):
        pltpu.make_async_copy(ref, ref, rsem.at[ri]).wait()

    barrier = pltpu.get_barrier_semaphore()
    for dx in range(4):
        for dy in range(ny):
            if dx or dy:
                to = dev(lax.rem(x + dx, 4), lax.rem(y + dy, ny), t)
                pl.semaphore_signal(barrier, inc=1, device_id=to, device_id_type=MESH)

    def greet(d, carry):
        to = dev(x, y, lax.rem(t + d, nt))
        pl.semaphore_signal(barrier, inc=1, device_id=to, device_id_type=MESH)
        return carry

    lax.fori_loop(1, nt, greet, 0)

    copy_table = local(slot_block, slot_table)
    copy_gv = local(grads, gv)
    copy_l = local(left_root.at[0], l2.at[lax.rem(x, 2)])
    copy_r = local(right_root.at[0], r2.at[xhalf])
    copy_lg = local(left_gram, lg)
    copy_rg = local(right_gram, rg)
    pl.semaphore_wait(barrier, 4 * ny - 1 + nt - 1)

    def fourth(k):
        return pl.ds(pl.multiple_of(lax.rem(k, 4) * 2 * cw, 2 * cw), 2 * cw)

    def cols(j, q, c):
        return pl.ds(pl.multiple_of(j * bs + q * 2 * cw + c * cw, cw), cw)

    rs1_r = [[[take("r") for _ in range(2)] for _ in range(2)] for _ in range(2)]
    rs2_r = [[take("r") for _ in range(2)] for _ in range(2)]

    def rs1_start(c):
        for w in (1, 0):
            si = [take("s") for _ in range(2)]

            def one(j, carry, w=w, si=si):
                for m, to_x in enumerate((xa, xb)):
                    q = xo if w == 1 else to_x
                    remote(
                        grads.at[m, :, :, cols(j, q, c)], rs1.at[c, m, w, j],
                        si[m], rs1_r[c][m][w], dev(to_x, y, t),
                    )
                return carry

            lax.fori_loop(0, jb, one, 0)
            for m in range(2):
                sends.append((rs1.at[c, m, w], si[m]))

    def rs2_start(c):
        for m, to_x in enumerate((xb, xa)):
            await_recv(rs1.at[c, m, 1], rs1_r[c][m][1])

            def one(j, carry, m=m, to_x=to_x):
                mine = gv[m, :, :, cols(j, to_x, c)].astype(F32)
                psend[c, m, j] = (mine + rs1[c, m, 1, j].astype(F32)).astype(BF16)
                return carry

            lax.fori_loop(0, jb, one, 0)
            si = take("s")
            remote(psend.at[c, m], rs2.at[c, m], si, rs2_r[c][m], dev(to_x, y, t))
            sends.append((psend.at[c, m], si))

    y1_r = [take("r") for _ in range(2)]
    t_r = [take("r") for _ in range(2)]
    y2_r = [take("r") for _ in range(2)]

    def y1_start(c):
        for m in range(2):
            await_recv(rs1.at[c, m, 0], rs1_r[c][m][0])
            await_recv(rs2.at[c, m], rs2_r[c][m])

            def one(j, carry, m=m):
                mine = gv[m, :, :, cols(j, x, c)].astype(F32)
                total = mine + rs1[c, m, 0, j].astype(F32) + rs2[c, m, j].astype(F32)
                ysum[c, :, m * jb + j] = total.astype(BF16)
                return carry

            lax.fori_loop(0, jb, one, 0)
        si = take("s")
        place = pl.ds(y * mj, mj)
        for d in y_steps:
            yy = lax.rem(y + d, ny)
            remote(ysum.at[c, yy], yrecv[c].at[place], si, y1_r[c], dev(x, yy, t))
        sends.append((ysum.at[c, pl.ds(0, ny - 1)], si))
        own["y1", c] = local(ysum.at[c, y], yrecv[c].at[place])

    def t_start(c):
        await_recv(yrecv[c].at[pl.ds(0, (ny - 1) * mj)], y1_r[c])
        own["y1", c].wait()
        si = take("s")

        def pick(tt):
            for yy in range(ny):
                b = slot_table[yy * nt + tt]
                row = lax.rem(lax.div(b, jb), ny)
                m = lax.div(b, jb * ny)
                tsend[c, tt, yy] = yrecv[c][row * mj + m * jb + lax.rem(b, jb)]

        def one(d, carry):
            tt = lax.rem(t + d, nt)
            pick(tt)
            remote(tsend.at[c, tt], trecv.at[c, t], si, t_r[c], dev(x, y, tt))
            return carry

        lax.fori_loop(1, nt, one, 0)
        pick(t)
        sends.append((tsend.at[c, pl.ds(0, nt - 1)], si))
        own["t", c] = local(tsend.at[c, t], trecv.at[c, t])

    def gcols(c):
        return pl.ds(c * cw, cw)

    def y2_start(c):
        await_recv(trecv.at[c, pl.ds(0, nt - 1)], t_r[c])
        own["t", c].wait()
        si = take("s")
        place = g.at[x, :, y, :, gcols(c)]
        for d in y_steps:
            yy = lax.rem(y + d, ny)
            remote(trecv.at[c, :, yy], place, si, y2_r[c], dev(x, yy, t))
        sends.append((trecv.at[c, :, pl.ds(0, ny - 1)], si))
        own["y2", c] = local(trecv.at[c, :, y], place)

    ag1_r = [[[take("r") for _ in range(2)] for _ in range(2)] for _ in range(2)]
    ag2_r = [[take("r") for _ in range(2)] for _ in range(2)]

    def gpart(q, h, c):
        return g.at[q, pl.ds(h * half, half), :, :, gcols(c)]

    def ag1_start(c):
        await_recv(g.at[x, :, pl.ds(0, ny - 1), :, gcols(c)], y2_r[c])
        own["y2", c].wait()
        for first in (True, False):
            for e, to_x in enumerate((xa, xb)):
                h = e if first else 1 - e
                part = gpart(x, h, c)
                si = take("s")
                remote(part, part, si, ag1_r[c][e][h], dev(to_x, y, t))
                sends.append((part, si))

    def ag2_start(c):
        for e, (source, to_x) in enumerate(((xa, xb), (xb, xa))):
            part = gpart(source, e, c)
            await_recv(part, ag1_r[c][e][e])
            si = take("s")
            remote(part, part, si, ag2_r[c][e], dev(to_x, y, t))
            sends.append((part, si))

    rs1_start(0)
    copy_table.wait()
    lanes = lax.broadcasted_iota(jnp.int32, place_row.shape, 1)

    def turn(k, row):
        at = lax.rem(k, nt) * ny + lax.div(k, nt)
        return jnp.where(lanes == slot_table[k], at, row)

    place_row[...] = lax.fori_loop(0, ny * nt, turn, jnp.zeros_like(lanes))
    copy_place = local(place_row, slot_place)
    copy_gv.wait()
    rs2_start(0)
    rs1_start(1)
    y1_start(0)
    rs2_start(1)
    l_s, r_s, l_r, r_r = take("s"), take("s"), take("r"), take("r")
    mine_l, mine_r = lax.rem(x, 2), xhalf
    for k in range(1, 4):
        square = fourth(xa + k)
        remote(
            left_root.at[0, :, square], l2.at[mine_l, :, square], l_s, l_r, dev(xa, y, t)
        )
        square = fourth(xb + k)
        remote(
            right_root.at[0, square], r2.at[mine_r, square], r_s, r_r, dev(xb, y, t)
        )
    l_bytes = l2.at[0, :, pl.ds(0, 6 * cw)]
    r_bytes = r2.at[0, pl.ds(0, 6 * cw)]
    sends.append((l_bytes, l_s))
    sends.append((r_bytes, r_s))
    t_start(0)
    y1_start(1)
    y2_start(0)
    t_start(1)
    copy_l.wait()
    l2[1 - mine_l, :, fourth(x)] = l2[mine_l, :, fourth(xa)].T
    copy_r.wait()
    r2[1 - mine_r, fourth(x)] = r2[mine_r, fourth(xb)].T
    ag1_start(0)
    ag2_start(0)
    y2_start(1)
    ag1_start(1)
    ag2_start(1)

    def block_cols(q):
        return g[q].reshape(bs, 2 * cw)

    def rows_times(q):
        part = dot(l2[...].reshape(bs // 2, bs), block_cols(q), ((1,), (0,)))
        nbuf[:, pl.ds(pl.multiple_of(q * 2 * cw, 2 * cw), 2 * cw)] = part.astype(BF16)

    await_recv(l_bytes, l_r)
    rows_times(x)
    for e, source in enumerate((xa, xb)):
        await_recv(gpart(source, 1 - e, 0), ag1_r[0][e][1 - e])
        await_recv(gpart(source, 1 - e, 1), ag1_r[1][e][1 - e])
        rows_times(source)
    for c in range(2):
        for e in range(2):
            await_recv(gpart(xo, e, c), ag2_r[c][e])
    rows_times(xo)

    await_recv(r_bytes, r_r)
    z, core = lax.div(t, 2), lax.rem(t, 2)
    quads = nt // 4
    a_s = [[take("s") for _ in range(2)] for _ in range(2)]
    a_r = [[take("r") for _ in range(2)] for _ in range(2)]

    def a_start(c):
        part = dot(nbuf[...], r2[c], ((1,), (0,))).astype(BF16)
        for h in range(2):
            pbuf[c, h] = part[:, h * cw : (h + 1) * cw].reshape(quads, 2, 4, rr, cw)
        place = pa.at[c, y, pair, pl.ds(xhalf * quads, quads)]
        for dx in (2, 1, 3, 0):
            for dy in (2, 1, 3, 0):
                xx, yy = lax.rem(x + dx, 4), lax.rem(y + dy, 4)
                src = pbuf.at[c, lax.div(yy, 2), :, lax.rem(yy + c, 2), xx]
                k = 0 if dx else 1
                if dx or dy:
                    remote(src, place, a_s[c][k], a_r[c][k], dev(xx, yy, t))
                else:
                    own["a", c] = local(src, place)
        for k in range(2):
            sends.append((a_bytes(c, k), a_s[c][k]))

    def a_bytes(c, k):
        return pa.at[c, pl.ds(0, 3), 0, pl.ds(0, quads)] if k else pa.at[c, pl.ds(0, 3)]

    b_s, b_r = take("s"), take("r")
    b_place = pb.at[pl.ds(t * 4, 4)]
    b_bytes = pb.at[pl.ds(0, (nt - 1) * 4)]

    def b_start(c):
        for k in range(2):
            await_recv(a_bytes(c, k), a_r[c][k])
        own["a", c].wait()

        def stripe(d, carry):
            zz = lax.rem(z + d, nt // 2)
            to = dev(x, y, 2 * zz + lax.rem(y + c, 2))
            remote(pa.at[c, :, :, zz], b_place, b_s, b_r, to)
            return carry

        lax.fori_loop(1, nt // 2, stripe, 0)

    a_start(0)
    a_start(1)
    copy_lg.wait()
    for q in range(4):
        rows = g[q, pl.ds(x * per, per)].reshape(bs // 4, 2 * cw)
        lg[0] += dot(rows, block_cols(q), ((1,), (1,)))
    b_start(0)
    b_start(1)
    here = lax.rem(core + y, 2)
    remote(pa.at[1 - here, :, :, z], b_place, b_s, b_r, dev(x, y, 2 * z + 1 - core))
    own["b"] = local(pa.at[here, :, :, z], b_place)
    sends.append((b_bytes, b_s))

    copy_rg.wait()
    turned = block_cols(x).T
    for q in range(4):
        part = pl.ds(q * 2 * cw, 2 * cw)
        rg[0, :, part] += dot(turned, block_cols(q), ((1,), (0,)))

    await_recv(b_bytes, b_r)
    own["b"].wait()
    copy_place.wait()

    def collect(yy):
        def one(j, carry):
            for m in range(2):
                csend[yy, m * jb + j] = pb[slot_place[0, (m * 4 + yy) * jb + j]]
            return carry

        lax.fori_loop(0, jb, one, 0)

    c_s = [take("s") for _ in range(4)]
    c_r = [take("r") for _ in range(4)]
    for d in y_steps:
        yy = lax.rem(y + d, 4)
        collect(yy)
        remote(csend.at[yy], cr.at[y], c_s[d], c_r[d], dev(x, yy, t))
        sends.append((csend.at[0], c_s[d]))
    collect(y)

    def lay(src, yy):
        c = lax.rem(core + yy, 2)
        for p in range(2):
            quarter = p + c * (3 - 2 * p)

            def one(j, carry, p=p, quarter=quarter):
                for m in range(2):
                    at = j * bs + quarter * 2 * cw + lax.div(yy, 2) * cw
                    upd[m, :, pl.ds(pl.multiple_of(at, cw), cw)] = src[yy, m * jb + j, p]
                return carry

            lax.fori_loop(0, jb, one, 0)

    lay(csend, y)
    for d in y_steps:
        yy = lax.rem(y - d + 4, 4)
        await_recv(cr.at[yy], c_r[d])
        lay(cr, yy)

    for ref, si in sends:
        pltpu.make_async_copy(ref, ref, ssem.at[si]).wait()
    assert counters["l"] <= N_LOCAL and counters["s"] <= N_SEND and counters["r"] <= N_RECV


def hand_on(*refs):
    sem = refs[-1]
    copies = [pltpu.make_async_copy(refs[i], refs[3 + i], sem.at[i]) for i in range(3)]
    for copy in copies:
        copy.start()
    for copy in copies:
        copy.wait()


def body(ny, grads, slot_block, left_gram, right_gram, left_root, right_root):
    owners = lax.axis_size("fsdp")
    nt = owners // ny
    bs = left_gram.shape[2]
    stripe, width = grads.shape[2], grads.shape[3]
    jb = width // bs
    mj = 2 * jb
    cw = bs // 8
    sr = stripe // ny
    rr = stripe // 4
    vm = pltpu.VMEM
    scratch = [
        vm((2, ny, sr, width), BF16),
        vm((2, 2, 2, jb, ny, sr, cw), BF16),
        vm((2, 2, jb, ny, sr, cw), BF16),
        vm((2, 2, jb, ny, sr, cw), BF16),
        vm((2, ny, mj, sr, cw), BF16),
        vm((ny * mj, sr, cw), BF16),
        vm((ny * mj, sr, cw), BF16),
        vm((2, nt, ny, sr, cw), BF16),
        vm((2, nt, ny, sr, cw), BF16),
        vm((4, nt, ny, sr, 2 * cw), BF16),
        vm((2, bs // 4, bs), BF16),
        vm((2, bs, 2 * cw), BF16),
        vm((bs // 2, bs), BF16),
        vm((2, 2, nt // 4, 2, 4, rr, cw), BF16),
        vm((2, ny, 2, nt // 2, rr, cw), BF16),
        vm((nt * ny, 2, rr, cw), BF16),
        vm((ny, mj, 2, rr, cw), BF16),
        vm((ny, mj, 2, rr, cw), BF16),
        vm((1, 128), jnp.int32),
        pltpu.SMEM((ny * nt,), jnp.int32),
        pltpu.SMEM((1, 128), jnp.int32),
        pltpu.SemaphoreType.DMA((N_LOCAL,)),
        pltpu.SemaphoreType.DMA((N_SEND,)),
        pltpu.SemaphoreType.DMA((N_RECV,)),
    ]
    whole = pl.BlockSpec(memory_space=pltpu.HBM)
    inside = pl.BlockSpec(memory_space=pltpu.VMEM)
    operands = (
        slot_block, grads.reshape(2, ny, sr, width), left_gram, right_gram, left_root, right_root
    )
    outs = pl.pallas_call(
        functools.partial(kernel, (ny, nt, jb, cw)),
        out_shape=(
            pltpu.VMEM(left_gram.shape, F32),
            pltpu.VMEM(right_gram.shape, F32),
            pltpu.VMEM((2, rr, width), BF16),
        ),
        in_specs=[whole, whole, whole, whole, whole, whole],
        out_specs=(inside,) * 3,
        scratch_shapes=scratch,
        compiler_params=pltpu.CompilerParams(
            collective_id=0, has_side_effects=True, vmem_limit_bytes=48 * 1024 * 1024
        ),
        cost_estimate=pl.CostEstimate(
            flops=5 * bs**3 // 2, bytes_accessed=12 * bs * bs, transcendentals=0
        ),
        name="shampoo",
    )(
        *(pltpu.with_memory_space_constraint(a, pltpu.HBM) for a in operands)
    )
    return pl.pallas_call(
        hand_on,
        out_shape=tuple(pltpu.HBM(a.shape, a.dtype) for a in outs),
        in_specs=[inside] * 3,
        out_specs=(whole,) * 3,
        scratch_shapes=[pltpu.SemaphoreType.DMA((3,))],
        name="hand_on",
    )(*(pltpu.with_memory_space_constraint(a, pltpu.VMEM) for a in outs))


def solution(mesh, ny=4):
    in_specs = (
        P("rep", None, "fsdp", None),
        P(),
        P("fsdp", "rep", None),
        P("fsdp", "rep", None),
        P("fsdp", "rep", None),
        P("fsdp", None, "rep"),
    )
    out_specs = (P("fsdp", "rep", None), P("fsdp", "rep", None), P(None, ("fsdp", "rep"), None))
    return jax.shard_map(
        functools.partial(body, ny), mesh=mesh, in_specs=in_specs, out_specs=out_specs,
        check_vma=False,
    )
```

```python
import functools

import jax
import jax.numpy as jnp
from jax import lax
from jax.experimental import pallas as pl
from jax.experimental.pallas import tpu as pltpu
from jax.sharding import PartitionSpec as P

MESH = pl.DeviceIdType.MESH
BF16 = jnp.bfloat16
F32 = jnp.float32
N_LOCAL, N_SEND, N_RECV = 20, 64, 64


def dot(a, b, dims):
    return lax.dot_general(a, b, (dims, ((), ())), preferred_element_type=F32)


def kernel(
    sizes,
    slot_block, grads, left_gram, right_gram, left_root, right_root,
    lg, rg, upd,
    gv, rs1, psend, rs2, ysum, yrecv0, yrecv1, tsend, g, l2, r2, nbuf, pbuf, pa, pb,
    csend, cr, place_row, slot_table, fetch, slot_place, lsem, ssem, rsem,
):
    ny, nt, jb, cw = sizes
    mj = 2 * jb
    bs = 8 * cw
    half = nt // 2
    per = nt // 4
    rr = bs // nt // 4
    yrecv = (yrecv0, yrecv1)
    s = lax.axis_index("fsdp")
    x = lax.axis_index("rep")
    y = lax.div(s, nt)
    t = lax.rem(s, nt)
    xa = x + 1 - 2 * lax.rem(x, 2)
    xb = 3 - x
    xo = lax.rem(x + 2, 4)
    xhalf = lax.div(x, 2)
    pair = jnp.minimum(x, xb)
    y_steps = (ny // 2, *[d for d in range(1, ny) if d != ny // 2])

    counters = {"l": 0, "s": 0, "r": 0}

    def take(kind):
        counters[kind] += 1
        return counters[kind] - 1

    sends = []
    own = {}

    def dev(xx, yy, tt):
        return (yy * nt + tt, xx)

    def remote(src, dst, si, ri, to):
        pltpu.make_async_remote_copy(
            src_ref=src, dst_ref=dst, send_sem=ssem.at[si], recv_sem=rsem.at[ri],
            device_id=to, device_id_type=MESH,
        ).start()

    def local(src, dst):
        copy = pltpu.make_async_copy(src, dst, lsem.at[take("l")])
        copy.start()
        return copy

    def await_recv(ref, ri):
        pltpu.make_async_copy(ref, ref, rsem.at[ri]).wait()

    barrier = pltpu.get_barrier_semaphore()
    for dx in range(4):
        for dy in range(ny):
            if dx or dy:
                to = dev(lax.rem(x + dx, 4), lax.rem(y + dy, ny), t)
                pl.semaphore_signal(barrier, inc=1, device_id=to, device_id_type=MESH)

    def greet(d, carry):
        to = dev(x, y, lax.rem(t + d, nt))
        pl.semaphore_signal(barrier, inc=1, device_id=to, device_id_type=MESH)
        return carry

    lax.fori_loop(1, nt, greet, 0)

    copy_table = local(slot_block, slot_table)
    copy_gv = local(grads, gv)
    copy_l = local(left_root.at[0], l2.at[lax.rem(x, 2)])
    copy_r = local(right_root.at[0], r2.at[xhalf])
    copy_lg = local(left_gram, lg)
    copy_rg = local(right_gram, rg)
    pl.semaphore_wait(barrier, 4 * ny - 1 + nt - 1)

    def fourth(k):
        return pl.ds(pl.multiple_of(lax.rem(k, 4) * 2 * cw, 2 * cw), 2 * cw)

    def outward(k, n):
        return n // 2 + lax.div(k + 1, 2) * (1 - 2 * lax.rem(k, 2))

    def cols(j, q, c):
        return pl.ds(pl.multiple_of(j * bs + q * 2 * cw + c * cw, cw), cw)

    rs1_r = [[[take("r") for _ in range(2)] for _ in range(2)] for _ in range(2)]
    rs2_r = [[take("r") for _ in range(2)] for _ in range(2)]

    def rs1_start(c):
        for w in (1, 0):
            si = [take("s") for _ in range(2)]

            def one(j, carry, w=w, si=si):
                for m, to_x in enumerate((xa, xb)):
                    q = xo if w == 1 else to_x
                    remote(
                        grads.at[m, :, :, cols(j, q, c)], rs1.at[c, m, w, j],
                        si[m], rs1_r[c][m][w], dev(to_x, y, t),
                    )
                return carry

            lax.fori_loop(0, jb, one, 0)
            for m in range(2):
                sends.append((rs1.at[c, m, w], si[m]))

    def rs2_start(c):
        for m, to_x in enumerate((xb, xa)):
            await_recv(rs1.at[c, m, 1], rs1_r[c][m][1])

            def one(j, carry, m=m, to_x=to_x):
                mine = gv[m, :, :, cols(j, to_x, c)].astype(F32)
                psend[c, m, j] = (mine + rs1[c, m, 1, j].astype(F32)).astype(BF16)
                return carry

            lax.fori_loop(0, jb, one, 0)
            si = take("s")
            remote(psend.at[c, m], rs2.at[c, m], si, rs2_r[c][m], dev(to_x, y, t))
            sends.append((psend.at[c, m], si))

    y1_r = [take("r") for _ in range(2)]
    t_r = [[take("r") for _ in range(2)] for _ in range(2)]

    def y1_start(c):
        for m in range(2):
            await_recv(rs1.at[c, m, 0], rs1_r[c][m][0])
            await_recv(rs2.at[c, m], rs2_r[c][m])

            def one(j, carry, m=m):
                mine = gv[m, :, :, cols(j, x, c)].astype(F32)
                total = mine + rs1[c, m, 0, j].astype(F32) + rs2[c, m, j].astype(F32)
                ysum[c, :, m * jb + j] = total.astype(BF16)
                return carry

            lax.fori_loop(0, jb, one, 0)
        si = take("s")
        place = pl.ds(y * mj, mj)
        for d in y_steps:
            yy = lax.rem(y + d, ny)
            remote(ysum.at[c, yy], yrecv[c].at[place], si, y1_r[c], dev(x, yy, t))
        sends.append((ysum.at[c, pl.ds(0, ny - 1)], si))
        own["y1", c] = local(ysum.at[c, y], yrecv[c].at[place])

    def t_bytes(c, k):
        return tsend.at[c, 0, pl.ds(0, 3)] if k else tsend.at[c, pl.ds(0, nt - 1)]

    def t_start(c):
        await_recv(yrecv[c].at[pl.ds(0, 3 * mj)], y1_r[c])
        own["y1", c].wait()
        si = [take("s") for _ in range(2)]
        place = g.at[x, t, y, :, gcols(c)]

        def pick(tt, dy):
            yy = lax.rem(y + dy, 4)
            tsend[c, tt, yy] = yrecv[c][fetch[yy * nt + tt]]
            return tsend.at[c, tt, yy], dev(x, yy, tt)

        def one(k, carry):
            tt = lax.rem(t + outward(k, nt), nt)
            for dy in (2, 1, 3, 0):
                src, to = pick(tt, dy)
                remote(src, place, si[0], t_r[c][0], to)
            return carry

        lax.fori_loop(0, nt - 1, one, 0)
        for dy in (2, 1, 3):
            src, to = pick(t, dy)
            remote(src, place, si[1], t_r[c][1], to)
        src, _ = pick(t, 0)
        own["t", c] = local(src, place)
        for k in range(2):
            sends.append((t_bytes(c, k), si[k]))

    def gcols(c):
        return pl.ds(c * cw, cw)

    ag1_r = [[[take("r") for _ in range(2)] for _ in range(2)] for _ in range(2)]
    ag2_r = [[take("r") for _ in range(2)] for _ in range(2)]

    def gpart(q, h, c):
        return g.at[q, pl.ds(h * half, half), :, :, gcols(c)]

    def ag1_start(c):
        for k in range(2):
            await_recv(t_bytes(c, k), t_r[c][k])
        own["t", c].wait()
        for first in (True, False):
            for e, to_x in enumerate((xa, xb)):
                h = e if first else 1 - e
                part = gpart(x, h, c)
                si = take("s")
                remote(part, part, si, ag1_r[c][e][h], dev(to_x, y, t))
                sends.append((part, si))

    def ag2_start(c):
        for e, (source, to_x) in enumerate(((xa, xb), (xb, xa))):
            part = gpart(source, e, c)
            await_recv(part, ag1_r[c][e][e])
            si = take("s")
            remote(part, part, si, ag2_r[c][e], dev(to_x, y, t))
            sends.append((part, si))

    rs1_start(0)
    copy_table.wait()
    lanes = lax.broadcasted_iota(jnp.int32, place_row.shape, 1)

    def turn(k, row):
        b = slot_table[k]
        fetch[k] = lax.rem(lax.div(b, jb), ny) * mj + lax.div(b, jb * ny) * jb + lax.rem(b, jb)
        at = lax.rem(k, nt) * ny + lax.div(k, nt)
        return jnp.where(lanes == b, at, row)

    place_row[...] = lax.fori_loop(0, ny * nt, turn, jnp.zeros_like(lanes))
    copy_place = local(place_row, slot_place)
    copy_gv.wait()
    rs2_start(0)
    rs1_start(1)
    y1_start(0)
    rs2_start(1)
    l_s, r_s, l_r, r_r = take("s"), take("s"), take("r"), take("r")
    mine_l, mine_r = lax.rem(x, 2), xhalf
    for k in range(1, 4):
        square = fourth(xa + k)
        remote(
            left_root.at[0, :, square], l2.at[mine_l, :, square], l_s, l_r, dev(xa, y, t)
        )
        square = fourth(xb + k)
        remote(
            right_root.at[0, square], r2.at[mine_r, square], r_s, r_r, dev(xb, y, t)
        )
    l_bytes = l2.at[0, :, pl.ds(0, 6 * cw)]
    r_bytes = r2.at[0, pl.ds(0, 6 * cw)]
    sends.append((l_bytes, l_s))
    sends.append((r_bytes, r_s))
    t_start(0)
    y1_start(1)
    t_start(1)
    copy_l.wait()
    l2[1 - mine_l, :, fourth(x)] = l2[mine_l, :, fourth(xa)].T
    copy_r.wait()
    r2[1 - mine_r, fourth(x)] = r2[mine_r, fourth(xb)].T
    ag1_start(0)
    ag2_start(0)
    ag1_start(1)
    ag2_start(1)

    def block_cols(q):
        return g[q].reshape(bs, 2 * cw)

    def rows_times(q):
        part = dot(l2[...].reshape(bs // 2, bs), block_cols(q), ((1,), (0,)))
        nbuf[:, pl.ds(pl.multiple_of(q * 2 * cw, 2 * cw), 2 * cw)] = part.astype(BF16)

    await_recv(l_bytes, l_r)
    rows_times(x)
    for e, source in enumerate((xa, xb)):
        await_recv(gpart(source, 1 - e, 0), ag1_r[0][e][1 - e])
        await_recv(gpart(source, 1 - e, 1), ag1_r[1][e][1 - e])
        rows_times(source)
    for c in range(2):
        for e in range(2):
            await_recv(gpart(xo, e, c), ag2_r[c][e])
    rows_times(xo)

    await_recv(r_bytes, r_r)
    z, core = lax.div(t, 2), lax.rem(t, 2)
    quads = nt // 4
    a_s = [[take("s") for _ in range(2)] for _ in range(2)]
    a_r = [[take("r") for _ in range(2)] for _ in range(2)]

    def a_start(c):
        part = dot(nbuf[...], r2[c], ((1,), (0,))).astype(BF16)
        for h in range(2):
            pbuf[c, h] = part[:, h * cw : (h + 1) * cw].reshape(quads, 2, 4, rr, cw)
        place = pa.at[c, y, pair, pl.ds(xhalf * quads, quads)]
        for dx in (2, 1, 3, 0):
            for dy in (2, 1, 3, 0):
                xx, yy = lax.rem(x + dx, 4), lax.rem(y + dy, 4)
                src = pbuf.at[c, lax.div(yy, 2), :, lax.rem(yy + c, 2), xx]
                k = 0 if dx else 1
                if dx or dy:
                    remote(src, place, a_s[c][k], a_r[c][k], dev(xx, yy, t))
                else:
                    own["a", c] = local(src, place)
        for k in range(2):
            sends.append((a_bytes(c, k), a_s[c][k]))

    def a_bytes(c, k):
        return pa.at[c, pl.ds(0, 3), 0, pl.ds(0, quads)] if k else pa.at[c, pl.ds(0, 3)]

    b_s, b_r = take("s"), take("r")
    b_place = pb.at[pl.ds(t * 4, 4)]
    b_bytes = pb.at[pl.ds(0, (nt - 1) * 4)]

    def b_start(c):
        for k in range(2):
            await_recv(a_bytes(c, k), a_r[c][k])
        own["a", c].wait()

        def stripe(k, carry):
            zz = lax.rem(z + outward(k, nt // 2), nt // 2)
            to = dev(x, y, 2 * zz + lax.rem(y + c, 2))
            remote(pa.at[c, :, :, zz], b_place, b_s, b_r, to)
            return carry

        lax.fori_loop(0, nt // 2 - 1, stripe, 0)

    a_start(0)
    a_start(1)
    copy_lg.wait()
    for q in range(4):
        rows = g[q, pl.ds(x * per, per)].reshape(bs // 4, 2 * cw)
        lg[0] += dot(rows, block_cols(q), ((1,), (1,)))
    b_start(0)
    b_start(1)
    here = lax.rem(core + y, 2)
    remote(pa.at[1 - here, :, :, z], b_place, b_s, b_r, dev(x, y, 2 * z + 1 - core))
    own["b"] = local(pa.at[here, :, :, z], b_place)
    sends.append((b_bytes, b_s))

    copy_rg.wait()
    turned = block_cols(x).T
    for q in range(4):
        part = pl.ds(q * 2 * cw, 2 * cw)
        rg[0, :, part] += dot(turned, block_cols(q), ((1,), (0,)))

    await_recv(b_bytes, b_r)
    own["b"].wait()
    copy_place.wait()

    def collect(yy):
        def one(j, carry):
            for m in range(2):
                csend[yy, m * jb + j] = pb[slot_place[0, (m * 4 + yy) * jb + j]]
            return carry

        lax.fori_loop(0, jb, one, 0)

    c_s = [take("s") for _ in range(4)]
    c_r = [take("r") for _ in range(4)]
    for d in y_steps:
        yy = lax.rem(y + d, 4)
        collect(yy)
        remote(csend.at[yy], cr.at[y], c_s[d], c_r[d], dev(x, yy, t))
        sends.append((csend.at[0], c_s[d]))
    collect(y)

    def lay(src, yy):
        c = lax.rem(core + yy, 2)
        for p in range(2):
            quarter = p + c * (3 - 2 * p)

            def one(j, carry, p=p, quarter=quarter):
                for m in range(2):
                    at = j * bs + quarter * 2 * cw + lax.div(yy, 2) * cw
                    upd[m, :, pl.ds(pl.multiple_of(at, cw), cw)] = src[yy, m * jb + j, p]
                return carry

            lax.fori_loop(0, jb, one, 0)

    lay(csend, y)
    for d in y_steps:
        yy = lax.rem(y - d + 4, 4)
        await_recv(cr.at[yy], c_r[d])
        lay(cr, yy)

    for ref, si in sends:
        pltpu.make_async_copy(ref, ref, ssem.at[si]).wait()
    assert counters["l"] <= N_LOCAL and counters["s"] <= N_SEND and counters["r"] <= N_RECV


def hand_on(*refs):
    sem = refs[-1]
    copies = [pltpu.make_async_copy(refs[i], refs[3 + i], sem.at[i]) for i in range(3)]
    for copy in copies:
        copy.start()
    for copy in copies:
        copy.wait()


def body(ny, grads, slot_block, left_gram, right_gram, left_root, right_root):
    owners = lax.axis_size("fsdp")
    nt = owners // ny
    bs = left_gram.shape[2]
    stripe, width = grads.shape[2], grads.shape[3]
    jb = width // bs
    mj = 2 * jb
    cw = bs // 8
    sr = stripe // ny
    rr = stripe // 4
    vm = pltpu.VMEM
    scratch = [
        vm((2, ny, sr, width), BF16),
        vm((2, 2, 2, jb, ny, sr, cw), BF16),
        vm((2, 2, jb, ny, sr, cw), BF16),
        vm((2, 2, jb, ny, sr, cw), BF16),
        vm((2, ny, mj, sr, cw), BF16),
        vm((ny * mj, sr, cw), BF16),
        vm((ny * mj, sr, cw), BF16),
        vm((2, nt, ny, sr, cw), BF16),
        vm((4, nt, ny, sr, 2 * cw), BF16),
        vm((2, bs // 4, bs), BF16),
        vm((2, bs, 2 * cw), BF16),
        vm((bs // 2, bs), BF16),
        vm((2, 2, nt // 4, 2, 4, rr, cw), BF16),
        vm((2, ny, 2, nt // 2, rr, cw), BF16),
        vm((nt * ny, 2, rr, cw), BF16),
        vm((ny, mj, 2, rr, cw), BF16),
        vm((ny, mj, 2, rr, cw), BF16),
        vm((1, 128), jnp.int32),
        pltpu.SMEM((ny * nt,), jnp.int32),
        pltpu.SMEM((ny * nt,), jnp.int32),
        pltpu.SMEM((1, 128), jnp.int32),
        pltpu.SemaphoreType.DMA((N_LOCAL,)),
        pltpu.SemaphoreType.DMA((N_SEND,)),
        pltpu.SemaphoreType.DMA((N_RECV,)),
    ]
    whole = pl.BlockSpec(memory_space=pltpu.HBM)
    inside = pl.BlockSpec(memory_space=pltpu.VMEM)
    operands = (
        slot_block, grads.reshape(2, ny, sr, width), left_gram, right_gram, left_root, right_root
    )
    outs = pl.pallas_call(
        functools.partial(kernel, (ny, nt, jb, cw)),
        out_shape=(
            pltpu.VMEM(left_gram.shape, F32),
            pltpu.VMEM(right_gram.shape, F32),
            pltpu.VMEM((2, rr, width), BF16),
        ),
        in_specs=[whole, whole, whole, whole, whole, whole],
        out_specs=(inside,) * 3,
        scratch_shapes=scratch,
        compiler_params=pltpu.CompilerParams(
            collective_id=0, has_side_effects=True, vmem_limit_bytes=48 * 1024 * 1024
        ),
        cost_estimate=pl.CostEstimate(
            flops=5 * bs**3 // 2, bytes_accessed=12 * bs * bs, transcendentals=0
        ),
        name="shampoo",
    )(
        *(pltpu.with_memory_space_constraint(a, pltpu.HBM) for a in operands)
    )
    return pl.pallas_call(
        hand_on,
        out_shape=tuple(pltpu.HBM(a.shape, a.dtype) for a in outs),
        in_specs=[inside] * 3,
        out_specs=(whole,) * 3,
        scratch_shapes=[pltpu.SemaphoreType.DMA((3,))],
        name="hand_on",
    )(*(pltpu.with_memory_space_constraint(a, pltpu.VMEM) for a in outs))


def solution(mesh, ny=4):
    in_specs = (
        P("rep", None, "fsdp", None),
        P(),
        P("fsdp", "rep", None),
        P("fsdp", "rep", None),
        P("fsdp", "rep", None),
        P("fsdp", None, "rep"),
    )
    out_specs = (P("fsdp", "rep", None), P("fsdp", "rep", None), P(None, ("fsdp", "rep"), None))
    return jax.shard_map(
        functools.partial(body, ny), mesh=mesh, in_specs=in_specs, out_specs=out_specs,
        check_vma=False,
    )
```

```python
import functools

import jax
import jax.numpy as jnp
from jax import lax
from jax.experimental import pallas as pl
from jax.experimental.pallas import tpu as pltpu
from jax.sharding import PartitionSpec as P

MESH = pl.DeviceIdType.MESH
BF16 = jnp.bfloat16
F32 = jnp.float32
N_LOCAL, N_SEND, N_RECV = 20, 64, 64


def dot(a, b, dims):
    return lax.dot_general(a, b, (dims, ((), ())), preferred_element_type=F32)


def kernel(
    sizes,
    slot_block, grads, left_gram, right_gram, left_root, right_root,
    lg, rg, upd,
    gv, rs1, psend, rs2, ysum, yrecv0, yrecv1, tsend, g, l2, r2, nbuf, total, pbuf, pa, pb0, pb1,
    csend, cr, place_row, slot_table, fetch, slot_place, lsem, ssem, rsem,
):
    ny, nt, jb, cw = sizes
    mj = 2 * jb
    bs = 8 * cw
    half = nt // 2
    per = nt // 4
    rr = bs // nt // 4
    yrecv = (yrecv0, yrecv1)
    s = lax.axis_index("fsdp")
    x = lax.axis_index("rep")
    y = lax.div(s, nt)
    t = lax.rem(s, nt)
    xa = x + 1 - 2 * lax.rem(x, 2)
    xb = 3 - x
    xo = lax.rem(x + 2, 4)
    xhalf = lax.div(x, 2)
    pair = jnp.minimum(x, xb)
    y_steps = (ny // 2, *[d for d in range(1, ny) if d != ny // 2])

    counters = {"l": 0, "s": 0, "r": 0}

    def take(kind):
        counters[kind] += 1
        return counters[kind] - 1

    sends = []
    own = {}

    def dev(xx, yy, tt):
        return (yy * nt + tt, xx)

    def remote(src, dst, si, ri, to):
        pltpu.make_async_remote_copy(
            src_ref=src, dst_ref=dst, send_sem=ssem.at[si], recv_sem=rsem.at[ri],
            device_id=to, device_id_type=MESH,
        ).start()

    def local(src, dst):
        copy = pltpu.make_async_copy(src, dst, lsem.at[take("l")])
        copy.start()
        return copy

    def await_recv(ref, ri):
        pltpu.make_async_copy(ref, ref, rsem.at[ri]).wait()

    barrier = pltpu.get_barrier_semaphore()
    for to in ((xa, y), (xb, y), *((x, lax.rem(y + d, 4)) for d in (1, 2, 3))):
        pl.semaphore_signal(barrier, inc=1, device_id=dev(*to, t), device_id_type=MESH)

    def greet(d, carry):
        to = dev(x, y, lax.rem(t + d, nt))
        pl.semaphore_signal(barrier, inc=1, device_id=to, device_id_type=MESH)
        return carry

    lax.fori_loop(1, nt, greet, 0)

    copy_table = local(slot_block, slot_table)
    copy_gv = local(grads, gv)
    copy_l = local(left_root.at[0], l2.at[lax.rem(x, 2)])
    copy_r = local(right_root.at[0], r2.at[xhalf])
    copy_lg = local(left_gram, lg)
    copy_rg = local(right_gram, rg)
    pl.semaphore_wait(barrier, 5 + nt - 1)

    def fourth(k):
        return pl.ds(pl.multiple_of(lax.rem(k, 4) * 2 * cw, 2 * cw), 2 * cw)

    def outward(k, n):
        return n // 2 + lax.div(k + 1, 2) * (1 - 2 * lax.rem(k, 2))

    def cols(j, q, c):
        return pl.ds(pl.multiple_of(j * bs + q * 2 * cw + c * cw, cw), cw)

    rs1_r = [[[take("r") for _ in range(2)] for _ in range(2)] for _ in range(2)]
    rs2_r = [[take("r") for _ in range(2)] for _ in range(2)]

    def rs1_start(c):
        for w in (1, 0):
            si = [take("s") for _ in range(2)]

            def one(j, carry, w=w, si=si):
                for m, to_x in enumerate((xa, xb)):
                    q = xo if w == 1 else to_x
                    remote(
                        grads.at[m, :, :, cols(j, q, c)], rs1.at[c, m, w, j],
                        si[m], rs1_r[c][m][w], dev(to_x, y, t),
                    )
                return carry

            lax.fori_loop(0, jb, one, 0)
            for m in range(2):
                sends.append((rs1.at[c, m, w], si[m]))

    def rs2_start(c):
        for m, to_x in enumerate((xb, xa)):
            await_recv(rs1.at[c, m, 1], rs1_r[c][m][1])

            def one(j, carry, m=m, to_x=to_x):
                mine = gv[m, :, :, cols(j, to_x, c)].astype(F32)
                psend[c, m, j] = (mine + rs1[c, m, 1, j].astype(F32)).astype(BF16)
                return carry

            lax.fori_loop(0, jb, one, 0, unroll=True)
            si = take("s")
            remote(psend.at[c, m], rs2.at[c, m], si, rs2_r[c][m], dev(to_x, y, t))
            sends.append((psend.at[c, m], si))

    y1_r = [take("r") for _ in range(2)]
    t_r = [[take("r") for _ in range(2)] for _ in range(2)]

    def y1_start(c):
        si = take("s")
        for m in range(2):
            await_recv(rs1.at[c, m, 0], rs1_r[c][m][0])
            await_recv(rs2.at[c, m], rs2_r[c][m])

            def one(j, carry, m=m):
                mine = gv[m, :, :, cols(j, x, c)].astype(F32)
                whole = mine + rs1[c, m, 0, j].astype(F32) + rs2[c, m, j].astype(F32)
                ysum[c, :, m * jb + j] = whole.astype(BF16)
                return carry

            lax.fori_loop(0, jb, one, 0, unroll=True)
            blocks = pl.ds(m * jb, jb)
            place = yrecv[c].at[pl.ds(y * mj + m * jb, jb)]
            for d in y_steps:
                yy = lax.rem(y + d, ny)
                remote(ysum.at[c, yy, blocks], place, si, y1_r[c], dev(x, yy, t))
            own["y1", c, m] = local(ysum.at[c, y, blocks], place)
        sends.append((ysum.at[c, pl.ds(0, ny - 1)], si))

    def t_bytes(c, k):
        return tsend.at[c, 0, pl.ds(0, 3)] if k else tsend.at[c, pl.ds(0, nt - 1)]

    def t_start(c):
        await_recv(yrecv[c].at[pl.ds(0, 3 * mj)], y1_r[c])
        for m in range(2):
            own["y1", c, m].wait()
        si = [take("s") for _ in range(2)]
        place = g.at[x, t, y, :, gcols(c)]

        def pick(tt, dy):
            yy = lax.rem(y + dy, 4)
            tsend[c, tt, yy] = yrecv[c][fetch[yy * nt + tt]]
            return tsend.at[c, tt, yy], dev(x, yy, tt)

        def one(k, carry):
            tt = lax.rem(t + outward(k, nt), nt)
            for dy in (2, 1, 3, 0):
                src, to = pick(tt, dy)
                remote(src, place, si[0], t_r[c][0], to)
            return carry

        lax.fori_loop(0, nt - 1, one, 0)
        for dy in (2, 1, 3):
            src, to = pick(t, dy)
            remote(src, place, si[1], t_r[c][1], to)
        src, _ = pick(t, 0)
        own["t", c] = local(src, place)
        for k in range(2):
            sends.append((t_bytes(c, k), si[k]))

    def gcols(c):
        return pl.ds(c * cw, cw)

    ag1_r = [[[take("r") for _ in range(2)] for _ in range(2)] for _ in range(2)]
    ag2_r = [[take("r") for _ in range(2)] for _ in range(2)]

    def gpart(q, h, c):
        return g.at[q, pl.ds(h * half, half), :, :, gcols(c)]

    def ag1_start(c):
        for k in range(2):
            await_recv(t_bytes(c, k), t_r[c][k])
        own["t", c].wait()
        for first in (True, False):
            for e, to_x in enumerate((xa, xb)):
                h = e if first else 1 - e
                part = gpart(x, h, c)
                si = take("s")
                remote(part, part, si, ag1_r[c][e][h], dev(to_x, y, t))
                sends.append((part, si))

    def ag2_start(c):
        for e, (source, to_x) in enumerate(((xa, xb), (xb, xa))):
            part = gpart(source, e, c)
            await_recv(part, ag1_r[c][e][e])
            si = take("s")
            remote(part, part, si, ag2_r[c][e], dev(to_x, y, t))
            sends.append((part, si))

    rs1_start(0)
    copy_table.wait()
    lanes = lax.broadcasted_iota(jnp.int32, place_row.shape, 1)

    def turn(k, row):
        b = slot_table[k]
        fetch[k] = lax.rem(lax.div(b, jb), ny) * mj + lax.div(b, jb * ny) * jb + lax.rem(b, jb)
        at = lax.rem(k, nt) * ny + lax.div(k, nt)
        return jnp.where(lanes == b, at, row)

    place_row[...] = lax.fori_loop(0, ny * nt, turn, jnp.zeros_like(lanes))
    copy_place = local(place_row, slot_place)
    copy_gv.wait()
    rs2_start(0)
    rs1_start(1)
    y1_start(0)
    rs2_start(1)
    l_s, r_s, l_r, r_r = take("s"), take("s"), take("r"), take("r")
    mine_l, mine_r = lax.rem(x, 2), xhalf
    for k in range(1, 4):
        square = fourth(xa + k)
        remote(
            left_root.at[0, :, square], l2.at[mine_l, :, square], l_s, l_r, dev(xa, y, t)
        )
        square = fourth(xb + k)
        remote(
            right_root.at[0, square], r2.at[mine_r, square], r_s, r_r, dev(xb, y, t)
        )
    l_bytes = l2.at[0, :, pl.ds(0, 6 * cw)]
    r_bytes = r2.at[0, pl.ds(0, 6 * cw)]
    sends.append((l_bytes, l_s))
    sends.append((r_bytes, r_s))
    t_start(0)
    y1_start(1)
    t_start(1)
    copy_l.wait()
    l2[1 - mine_l, :, fourth(x)] = l2[mine_l, :, fourth(xa)].T
    copy_r.wait()
    r2[1 - mine_r, fourth(x)] = r2[mine_r, fourth(xb)].T
    ag1_start(0)
    ag2_start(0)
    ag1_start(1)

    def block_cols(q):
        return g[q].reshape(bs, 2 * cw)

    def rows_times(q):
        part = dot(l2[...].reshape(bs // 2, bs), block_cols(q), ((1,), (0,)))
        return part.astype(BF16)

    def product(c, q):
        return dot(nbuf[...], r2[c, fourth(q)], ((1,), (0,)))

    await_recv(l_bytes, l_r)
    await_recv(r_bytes, r_r)
    nbuf[...] = rows_times(x)
    for c in range(2):
        total[c] = product(c, x)
    ag2_start(1)
    for e, source in enumerate((xa, xb)):
        await_recv(gpart(source, 1 - e, 0), ag1_r[0][e][1 - e])
        await_recv(gpart(source, 1 - e, 1), ag1_r[1][e][1 - e])
        nbuf[...] = rows_times(source)
        for c in range(2):
            total[c] += product(c, source)
    for c in range(2):
        for e in range(2):
            await_recv(gpart(xo, e, c), ag2_r[c][e])
    nbuf[...] = rows_times(xo)

    z, core = lax.div(t, 2), lax.rem(t, 2)
    quads = nt // 4
    batches = (min(2, quads), 1)
    a_s = [[[take("s") for _ in range(2)] for _ in range(n)] for n in batches]
    a_r = [[[take("r") for _ in range(2)] for _ in range(n)] for n in batches]

    def a_start(c):
        part = (total[c] + product(c, xo)).astype(BF16)
        for h in range(2):
            pbuf[c, h] = part[:, h * cw : (h + 1) * cw].reshape(quads, 2, 4, rr, cw)
        n = quads // batches[c]
        for i in range(batches[c]):
            place = pa.at[c, y, pair, pl.ds(xhalf * quads + i * n, n)]
            for dx in (2, 1, 3, 0):
                for dy in (2, 1, 3, 0):
                    xx, yy = lax.rem(x + dx, 4), lax.rem(y + dy, 4)
                    tp = lax.rem(yy + c, 2)
                    src = pbuf.at[c, lax.div(yy, 2), pl.ds(i * n, n), tp, xx]
                    k = 0 if dx else 1
                    if dx or dy:
                        remote(src, place, a_s[c][i][k], a_r[c][i][k], dev(xx, yy, t))
                    else:
                        own["a", c, i] = local(src, place)
            for k in range(2):
                sends.append((a_bytes(c, k), a_s[c][i][k]))

    def a_bytes(c, k):
        n = quads // batches[c]
        return pa.at[c, pl.ds(0, 3), 0, pl.ds(0, n)] if k else pa.at[c, pl.ds(0, 3), :, pl.ds(0, 2 * n)]

    pb = (pb0, pb1)
    b_s = [take("s") for _ in range(2)]
    b_r = [take("r") for _ in range(2)]
    b_place = pl.ds(t * 4, 4)
    b_bytes = pl.ds(0, (nt - 1) * 4)

    def b_start(c, i):
        for k in range(2):
            await_recv(a_bytes(c, k), a_r[c][i][k])
        own["a", c, i].wait()
        n = quads // batches[c]
        for p in range(2):

            def stripe(k, carry, p=p):
                if batches[c] == 1:
                    zz = lax.rem(z + outward(k, nt // 2), nt // 2)
                else:
                    zz = lax.rem(k, 2) * quads + i * n + lax.div(k, 2)

                @pl.when(zz != z)
                def _():
                    to = dev(x, y, 2 * zz + lax.rem(y + c, 2))
                    remote(pa.at[c, :, p, zz], pb[p].at[b_place], b_s[p], b_r[p], to)

                return carry

            lax.fori_loop(0, 2 * n, stripe, 0)

    a_start(0)
    a_start(1)
    for i in range(batches[0]):
        b_start(0, i)
    copy_lg.wait()
    for q in range(4):
        rows = g[q, pl.ds(x * per, per)].reshape(bs // 4, 2 * cw)
        lg[0] += dot(rows, block_cols(q), ((1,), (1,)))
    b_start(1, 0)
    here = lax.rem(core + y, 2)
    for p in range(2):
        to = dev(x, y, 2 * z + 1 - core)
        remote(pa.at[1 - here, :, p, z], pb[p].at[b_place], b_s[p], b_r[p], to)
        own["b", p] = local(pa.at[here, :, p, z], pb[p].at[b_place])
        sends.append((pb[p].at[b_bytes], b_s[p]))

    copy_rg.wait()
    turned = block_cols(x).T
    for q in range(4):
        part = pl.ds(q * 2 * cw, 2 * cw)
        rg[0, :, part] += dot(turned, block_cols(q), ((1,), (0,)))

    copy_place.wait()

    def collect(p, yy):
        def one(j, carry):
            for m in range(2):
                csend[p, yy, m * jb + j] = pb[p][slot_place[0, (m * 4 + yy) * jb + j]]
            return carry

        lax.fori_loop(0, jb, one, 0, unroll=True)

    c_s = [[take("s") for _ in range(4)] for _ in range(2)]
    c_r = [[take("r") for _ in range(4)] for _ in range(2)]
    for p in range(2):
        await_recv(pb[p].at[b_bytes], b_r[p])
        own["b", p].wait()
        for d in y_steps:
            yy = lax.rem(y + d, 4)
            collect(p, yy)
            remote(csend.at[p, yy], cr.at[p, y], c_s[p][d], c_r[p][d], dev(x, yy, t))
            sends.append((csend.at[p, 0], c_s[p][d]))

    def lay(src, p, yy):
        quarter = p + lax.rem(core + yy, 2) * (3 - 2 * p)

        def one(j, carry):
            for m in range(2):
                at = j * bs + quarter * 2 * cw + lax.div(yy, 2) * cw
                upd[m, :, pl.ds(pl.multiple_of(at, cw), cw)] = src[p, yy, m * jb + j]
            return carry

        lax.fori_loop(0, jb, one, 0, unroll=True)

    for p in range(2):
        collect(p, y)
        lay(csend, p, y)
    for p in range(2):
        for d in y_steps:
            yy = lax.rem(y - d + 4, 4)
            await_recv(cr.at[p, yy], c_r[p][d])
            lay(cr, p, yy)

    for ref, si in sends:
        pltpu.make_async_copy(ref, ref, ssem.at[si]).wait()
    assert counters["l"] <= N_LOCAL and counters["s"] <= N_SEND and counters["r"] <= N_RECV


def hand_on(*refs):
    sem = refs[-1]
    copies = [pltpu.make_async_copy(refs[i], refs[3 + i], sem.at[i]) for i in range(3)]
    for copy in copies:
        copy.start()
    for copy in copies:
        copy.wait()


def body(ny, grads, slot_block, left_gram, right_gram, left_root, right_root):
    owners = lax.axis_size("fsdp")
    nt = owners // ny
    bs = left_gram.shape[2]
    stripe, width = grads.shape[2], grads.shape[3]
    jb = width // bs
    mj = 2 * jb
    cw = bs // 8
    sr = stripe // ny
    rr = stripe // 4
    vm = pltpu.VMEM
    scratch = [
        vm((2, ny, sr, width), BF16),
        vm((2, 2, 2, jb, ny, sr, cw), BF16),
        vm((2, 2, jb, ny, sr, cw), BF16),
        vm((2, 2, jb, ny, sr, cw), BF16),
        vm((2, ny, mj, sr, cw), BF16),
        vm((ny * mj, sr, cw), BF16),
        vm((ny * mj, sr, cw), BF16),
        vm((2, nt, ny, sr, cw), BF16),
        vm((4, nt, ny, sr, 2 * cw), BF16),
        vm((2, bs // 4, bs), BF16),
        vm((2, bs, 2 * cw), BF16),
        vm((bs // 2, 2 * cw), BF16),
        vm((2, bs // 2, 2 * cw), F32),
        vm((2, 2, nt // 4, 2, 4, rr, cw), BF16),
        vm((2, ny, 2, nt // 2, rr, cw), BF16),
        vm((nt * ny, rr, cw), BF16),
        vm((nt * ny, rr, cw), BF16),
        vm((2, ny, mj, rr, cw), BF16),
        vm((2, ny, mj, rr, cw), BF16),
        vm((1, 128), jnp.int32),
        pltpu.SMEM((ny * nt,), jnp.int32),
        pltpu.SMEM((ny * nt,), jnp.int32),
        pltpu.SMEM((1, 128), jnp.int32),
        pltpu.SemaphoreType.DMA((N_LOCAL,)),
        pltpu.SemaphoreType.DMA((N_SEND,)),
        pltpu.SemaphoreType.DMA((N_RECV,)),
    ]
    whole = pl.BlockSpec(memory_space=pltpu.HBM)
    inside = pl.BlockSpec(memory_space=pltpu.VMEM)
    operands = (
        slot_block, grads.reshape(2, ny, sr, width), left_gram, right_gram, left_root, right_root
    )
    outs = pl.pallas_call(
        functools.partial(kernel, (ny, nt, jb, cw)),
        out_shape=(
            pltpu.VMEM(left_gram.shape, F32),
            pltpu.VMEM(right_gram.shape, F32),
            pltpu.VMEM((2, rr, width), BF16),
        ),
        in_specs=[whole, whole, whole, whole, whole, whole],
        out_specs=(inside,) * 3,
        scratch_shapes=scratch,
        compiler_params=pltpu.CompilerParams(
            collective_id=0, has_side_effects=True, vmem_limit_bytes=48 * 1024 * 1024
        ),
        cost_estimate=pl.CostEstimate(
            flops=5 * bs**3 // 2, bytes_accessed=12 * bs * bs, transcendentals=0
        ),
        name="shampoo",
    )(
        *(pltpu.with_memory_space_constraint(a, pltpu.HBM) for a in operands)
    )
    return pl.pallas_call(
        hand_on,
        out_shape=tuple(pltpu.HBM(a.shape, a.dtype) for a in outs),
        in_specs=[inside] * 3,
        out_specs=(whole,) * 3,
        scratch_shapes=[pltpu.SemaphoreType.DMA((3,))],
        name="hand_on",
    )(*(pltpu.with_memory_space_constraint(a, pltpu.VMEM) for a in outs))


def solution(mesh, ny=4):
    in_specs = (
        P("rep", None, "fsdp", None),
        P(),
        P("fsdp", "rep", None),
        P("fsdp", "rep", None),
        P("fsdp", "rep", None),
        P("fsdp", None, "rep"),
    )
    out_specs = (P("fsdp", "rep", None), P("fsdp", "rep", None), P(None, ("fsdp", "rep"), None))
    return jax.shard_map(
        functools.partial(body, ny), mesh=mesh, in_specs=in_specs, out_specs=out_specs,
        check_vma=False,
    )
```

```python
import functools

import jax
import jax.numpy as jnp
from jax import lax
from jax.experimental import pallas as pl
from jax.experimental.pallas import tpu as pltpu
from jax.sharding import PartitionSpec as P

MESH = pl.DeviceIdType.MESH
BF16 = jnp.bfloat16
F32 = jnp.float32
N_LOCAL, N_SEND, N_RECV = 20, 64, 64


def dot(a, b, dims):
    return lax.dot_general(a, b, (dims, ((), ())), preferred_element_type=F32)


def kernel(
    sizes,
    slot_block, grads, left_gram, right_gram, left_root, right_root,
    lg, rg, upd,
    gv, rs1, psend, rs2, ysum, yrecv0, yrecv1, tsend, g, l2, r2, nbuf, total, pbuf, pa, pb0, pb1,
    csend, cr, place_row, slot_table, fetch, slot_place, lsem, ssem, rsem,
):
    ny, nt, jb, cw = sizes
    mj = 2 * jb
    bs = 8 * cw
    half = nt // 2
    per = nt // 4
    rr = bs // nt // 4
    yrecv = (yrecv0, yrecv1)
    s = lax.axis_index("fsdp")
    x = lax.axis_index("rep")
    y = lax.div(s, nt)
    t = lax.rem(s, nt)
    xa = x + 1 - 2 * lax.rem(x, 2)
    xb = 3 - x
    xo = lax.rem(x + 2, 4)
    xhalf = lax.div(x, 2)
    pair = jnp.minimum(x, xb)
    y_steps = (ny // 2, *[d for d in range(1, ny) if d != ny // 2])

    counters = {"l": 0, "s": 0, "r": 0}

    def take(kind):
        counters[kind] += 1
        return counters[kind] - 1

    sends = []
    own = {}

    def dev(xx, yy, tt):
        return (yy * nt + tt, xx)

    def remote(src, dst, si, ri, to):
        pltpu.make_async_remote_copy(
            src_ref=src, dst_ref=dst, send_sem=ssem.at[si], recv_sem=rsem.at[ri],
            device_id=to, device_id_type=MESH,
        ).start()

    def local(src, dst):
        copy = pltpu.make_async_copy(src, dst, lsem.at[take("l")])
        copy.start()
        return copy

    def await_recv(ref, ri):
        pltpu.make_async_copy(ref, ref, rsem.at[ri]).wait()

    barrier = pltpu.get_barrier_semaphore()
    for to in ((xa, y), (xb, y), *((x, lax.rem(y + d, 4)) for d in (1, 2, 3))):
        pl.semaphore_signal(barrier, inc=1, device_id=dev(*to, t), device_id_type=MESH)

    def greet(d, carry):
        to = dev(x, y, lax.rem(t + d, nt))
        pl.semaphore_signal(barrier, inc=1, device_id=to, device_id_type=MESH)
        return carry

    lax.fori_loop(1, nt, greet, 0)

    copy_table = local(slot_block, slot_table)
    copy_gv = local(grads, gv)
    copy_l = local(left_root.at[0], l2.at[lax.rem(x, 2)])
    copy_r = local(right_root.at[0], r2.at[xhalf])
    copy_lg = local(left_gram, lg)
    copy_rg = local(right_gram, rg)
    pl.semaphore_wait(barrier, 5 + nt - 1)

    def fourth(k):
        return pl.ds(pl.multiple_of(lax.rem(k, 4) * 2 * cw, 2 * cw), 2 * cw)

    def outward(k, n):
        return n // 2 + lax.div(k + 1, 2) * (1 - 2 * lax.rem(k, 2))

    def cols(j, q, c):
        return pl.ds(pl.multiple_of(j * bs + q * 2 * cw + c * cw, cw), cw)

    rs1_r = [[[take("r") for _ in range(2)] for _ in range(2)] for _ in range(2)]
    rs2_r = [[take("r") for _ in range(2)] for _ in range(2)]

    def rs1_start(c):
        for w in (1, 0):
            si = [take("s") for _ in range(2)]

            def one(j, carry, w=w, si=si):
                for m, to_x in enumerate((xa, xb)):
                    q = xo if w == 1 else to_x
                    remote(
                        grads.at[m, :, :, cols(j, q, c)], rs1.at[c, m, w, j],
                        si[m], rs1_r[c][m][w], dev(to_x, y, t),
                    )
                return carry

            lax.fori_loop(0, jb, one, 0)
            for m in range(2):
                sends.append((rs1.at[c, m, w], si[m]))

    def rs2_start(c):
        for m, to_x in enumerate((xb, xa)):
            await_recv(rs1.at[c, m, 1], rs1_r[c][m][1])

            def one(j, carry, m=m, to_x=to_x):
                mine = gv[m, :, :, cols(j, to_x, c)].astype(F32)
                psend[c, m, j] = (mine + rs1[c, m, 1, j].astype(F32)).astype(BF16)
                return carry

            lax.fori_loop(0, jb, one, 0, unroll=True)
            si = take("s")
            remote(psend.at[c, m], rs2.at[c, m], si, rs2_r[c][m], dev(to_x, y, t))
            sends.append((psend.at[c, m], si))

    y1_r = [take("r") for _ in range(2)]
    t_r = [[take("r") for _ in range(2)] for _ in range(2)]

    def y1_start(c):
        si = take("s")
        for m in range(2):
            await_recv(rs1.at[c, m, 0], rs1_r[c][m][0])
            await_recv(rs2.at[c, m], rs2_r[c][m])

            def one(j, carry, m=m):
                mine = gv[m, :, :, cols(j, x, c)].astype(F32)
                whole = mine + rs1[c, m, 0, j].astype(F32) + rs2[c, m, j].astype(F32)
                ysum[c, :, m * jb + j] = whole.astype(BF16)
                return carry

            lax.fori_loop(0, jb, one, 0, unroll=True)
            blocks = pl.ds(m * jb, jb)
            place = yrecv[c].at[pl.ds(y * mj + m * jb, jb)]
            for d in y_steps:
                yy = lax.rem(y + d, ny)
                remote(ysum.at[c, yy, blocks], place, si, y1_r[c], dev(x, yy, t))
            own["y1", c, m] = local(ysum.at[c, y, blocks], place)
        sends.append((ysum.at[c, pl.ds(0, ny - 1)], si))

    def t_bytes(c, k):
        return tsend.at[c, 0, pl.ds(0, 3)] if k else tsend.at[c, pl.ds(0, nt - 1)]

    def t_start(c):
        await_recv(yrecv[c].at[pl.ds(0, 3 * mj)], y1_r[c])
        for m in range(2):
            own["y1", c, m].wait()
        si = [take("s") for _ in range(2)]
        place = g.at[x, t, y, :, gcols(c)]

        def pick(tt, dy):
            yy = lax.rem(y + dy, 4)
            tsend[c, tt, yy] = yrecv[c][fetch[yy * nt + tt]]
            return tsend.at[c, tt, yy], dev(x, yy, tt)

        def one(k, carry):
            tt = lax.rem(t + outward(k, nt), nt)
            for dy in (2, 1, 3, 0):
                src, to = pick(tt, dy)
                remote(src, place, si[0], t_r[c][0], to)
            return carry

        lax.fori_loop(0, nt - 1, one, 0)
        for dy in (2, 1, 3):
            src, to = pick(t, dy)
            remote(src, place, si[1], t_r[c][1], to)
        src, _ = pick(t, 0)
        own["t", c] = local(src, place)
        for k in range(2):
            sends.append((t_bytes(c, k), si[k]))

    def gcols(c):
        return pl.ds(c * cw, cw)

    ag1_r = [[[take("r") for _ in range(2)] for _ in range(2)] for _ in range(2)]
    ag2_r = [[take("r") for _ in range(2)] for _ in range(2)]

    def gpart(q, h, c):
        return g.at[q, pl.ds(h * half, half), :, :, gcols(c)]

    def ag1_start(c):
        for k in range(2):
            await_recv(t_bytes(c, k), t_r[c][k])
        own["t", c].wait()
        for first in (True, False):
            for e, to_x in enumerate((xa, xb)):
                h = e if first else 1 - e
                part = gpart(x, h, c)
                si = take("s")
                remote(part, part, si, ag1_r[c][e][h], dev(to_x, y, t))
                sends.append((part, si))

    def ag2_start(c):
        for e, (source, to_x) in enumerate(((xa, xb), (xb, xa))):
            part = gpart(source, e, c)
            await_recv(part, ag1_r[c][e][e])
            si = take("s")
            remote(part, part, si, ag2_r[c][e], dev(to_x, y, t))
            sends.append((part, si))

    rs1_start(0)
    copy_table.wait()
    lanes = lax.broadcasted_iota(jnp.int32, place_row.shape, 1)

    def turn(k, row):
        b = slot_table[k]
        fetch[k] = lax.rem(lax.div(b, jb), ny) * mj + lax.div(b, jb * ny) * jb + lax.rem(b, jb)
        at = lax.rem(k, nt) * ny + lax.div(k, nt)
        return jnp.where(lanes == b, at, row)

    place_row[...] = lax.fori_loop(0, ny * nt, turn, jnp.zeros_like(lanes))
    copy_place = local(place_row, slot_place)
    copy_gv.wait()
    rs2_start(0)
    rs1_start(1)
    y1_start(0)
    rs2_start(1)
    l_s, r_s, l_r, r_r = take("s"), take("s"), take("r"), take("r")
    mine_l, mine_r = lax.rem(x, 2), xhalf
    for k in range(1, 4):
        square = fourth(xa + k)
        remote(
            left_root.at[0, :, square], l2.at[mine_l, :, square], l_s, l_r, dev(xa, y, t)
        )
        square = fourth(xb + k)
        remote(
            right_root.at[0, square], r2.at[mine_r, square], r_s, r_r, dev(xb, y, t)
        )
    l_bytes = l2.at[0, :, pl.ds(0, 6 * cw)]
    r_bytes = r2.at[0, pl.ds(0, 6 * cw)]
    sends.append((l_bytes, l_s))
    sends.append((r_bytes, r_s))
    t_start(0)
    y1_start(1)
    t_start(1)
    copy_l.wait()
    l2[1 - mine_l, :, fourth(x)] = l2[mine_l, :, fourth(xa)].T
    copy_r.wait()
    r2[1 - mine_r, fourth(x)] = r2[mine_r, fourth(xb)].T
    ag1_start(0)
    ag2_start(0)
    ag1_start(1)

    def block_cols(q):
        return g[q].reshape(bs, 2 * cw)

    def rows_times(q):
        part = dot(l2[...].reshape(bs // 2, bs), block_cols(q), ((1,), (0,)))
        return part.astype(BF16)

    def product(c, q):
        return dot(nbuf[...], r2[c, fourth(q)], ((1,), (0,)))

    await_recv(l_bytes, l_r)
    await_recv(r_bytes, r_r)
    nbuf[...] = rows_times(x)
    for c in range(2):
        total[c] = product(c, x)
    ag2_start(1)
    for e, source in enumerate((xa, xb)):
        await_recv(gpart(source, 1 - e, 0), ag1_r[0][e][1 - e])
        await_recv(gpart(source, 1 - e, 1), ag1_r[1][e][1 - e])
        nbuf[...] = rows_times(source)
        for c in range(2):
            total[c] += product(c, source)
    for c in range(2):
        for e in range(2):
            await_recv(gpart(xo, e, c), ag2_r[c][e])

    z, core = lax.div(t, 2), lax.rem(t, 2)
    quads = nt // 4
    batches = (min(2, quads), 1)
    a_s = [[[take("s") for _ in range(2)] for _ in range(n)] for n in batches]
    a_r = [[[take("r") for _ in range(2)] for _ in range(n)] for n in batches]

    def a_start(c):
        n = quads // batches[c]
        size = bs // 2 // batches[c]
        for i in range(batches[c]):
            rows = pl.ds(i * size, size)
            if c == 0:
                left = l2[...].reshape(bs // 2, bs)[i * size : (i + 1) * size]
                nbuf[rows] = dot(left, block_cols(xo), ((1,), (0,))).astype(BF16)
            last = dot(nbuf[rows], r2[c, fourth(xo)], ((1,), (0,)))
            part = (total[c, rows] + last).astype(BF16)
            for h in range(2):
                piece = part[:, h * cw : (h + 1) * cw].reshape(n, 2, 4, rr, cw)
                pbuf[c, h, pl.ds(i * n, n)] = piece
            place = pa.at[c, y, pair, pl.ds(xhalf * quads + i * n, n)]
            for dx in (2, 1, 3, 0):
                for dy in (2, 1, 3, 0):
                    xx, yy = lax.rem(x + dx, 4), lax.rem(y + dy, 4)
                    tp = lax.rem(yy + c, 2)
                    src = pbuf.at[c, lax.div(yy, 2), pl.ds(i * n, n), tp, xx]
                    k = 0 if dx else 1
                    if dx or dy:
                        remote(src, place, a_s[c][i][k], a_r[c][i][k], dev(xx, yy, t))
                    else:
                        own["a", c, i] = local(src, place)
            for k in range(2):
                sends.append((a_bytes(c, k), a_s[c][i][k]))

    def a_bytes(c, k):
        n = quads // batches[c]
        return pa.at[c, pl.ds(0, 3), 0, pl.ds(0, n)] if k else pa.at[c, pl.ds(0, 3), :, pl.ds(0, 2 * n)]

    pb = (pb0, pb1)
    b_s = [take("s") for _ in range(2)]
    b_r = [take("r") for _ in range(2)]
    b_place = pl.ds(t * 4, 4)
    b_bytes = pl.ds(0, (nt - 1) * 4)

    def b_start(c, i):
        for k in range(2):
            await_recv(a_bytes(c, k), a_r[c][i][k])
        own["a", c, i].wait()
        n = quads // batches[c]
        for p in range(2):

            def stripe(k, carry, p=p):
                if batches[c] == 1:
                    zz = lax.rem(z + outward(k, nt // 2), nt // 2)
                else:
                    j = lax.rem(k + z, 2 * n)
                    zz = lax.rem(j, 2) * quads + i * n + lax.div(j, 2)

                @pl.when(zz != z)
                def _():
                    to = dev(x, y, 2 * zz + lax.rem(y + c, 2))
                    remote(pa.at[c, :, p, zz], pb[p].at[b_place], b_s[p], b_r[p], to)

                return carry

            lax.fori_loop(0, 2 * n, stripe, 0)

    a_start(0)
    a_start(1)
    for i in range(batches[0]):
        b_start(0, i)
    copy_lg.wait()
    for q in range(4):
        rows = g[q, pl.ds(x * per, per)].reshape(bs // 4, 2 * cw)
        lg[0] += dot(rows, block_cols(q), ((1,), (1,)))
    b_start(1, 0)
    here = lax.rem(core + y, 2)
    for p in range(2):
        to = dev(x, y, 2 * z + 1 - core)
        remote(pa.at[1 - here, :, p, z], pb[p].at[b_place], b_s[p], b_r[p], to)
        own["b", p] = local(pa.at[here, :, p, z], pb[p].at[b_place])
        sends.append((pb[p].at[b_bytes], b_s[p]))

    copy_rg.wait()
    turned = block_cols(x).T
    for q in range(4):
        part = pl.ds(q * 2 * cw, 2 * cw)
        rg[0, :, part] += dot(turned, block_cols(q), ((1,), (0,)))

    copy_place.wait()

    def collect(p, yy):
        def one(j, carry):
            for m in range(2):
                csend[p, yy, m * jb + j] = pb[p][slot_place[0, (m * 4 + yy) * jb + j]]
            return carry

        lax.fori_loop(0, jb, one, 0, unroll=True)

    c_s = [[take("s") for _ in range(4)] for _ in range(2)]
    c_r = [[take("r") for _ in range(4)] for _ in range(2)]
    for p in range(2):
        await_recv(pb[p].at[b_bytes], b_r[p])
        own["b", p].wait()
        for d in y_steps:
            yy = lax.rem(y + d, 4)
            collect(p, yy)
            remote(csend.at[p, yy], cr.at[p, y], c_s[p][d], c_r[p][d], dev(x, yy, t))
            sends.append((csend.at[p, 0], c_s[p][d]))

    def lay(src, p, yy):
        quarter = p + lax.rem(core + yy, 2) * (3 - 2 * p)

        def one(j, carry):
            for m in range(2):
                at = j * bs + quarter * 2 * cw + lax.div(yy, 2) * cw
                upd[m, :, pl.ds(pl.multiple_of(at, cw), cw)] = src[p, yy, m * jb + j]
            return carry

        lax.fori_loop(0, jb, one, 0, unroll=True)

    for p in range(2):
        collect(p, y)
        lay(csend, p, y)
    for p in range(2):
        for d in y_steps:
            yy = lax.rem(y - d + 4, 4)
            await_recv(cr.at[p, yy], c_r[p][d])
            lay(cr, p, yy)

    for ref, si in sends:
        pltpu.make_async_copy(ref, ref, ssem.at[si]).wait()
    assert counters["l"] <= N_LOCAL and counters["s"] <= N_SEND and counters["r"] <= N_RECV


def hand_on(*refs):
    sem = refs[-1]
    copies = [pltpu.make_async_copy(refs[i], refs[3 + i], sem.at[i]) for i in range(3)]
    for copy in copies:
        copy.start()
    for copy in copies:
        copy.wait()


def body(ny, grads, slot_block, left_gram, right_gram, left_root, right_root):
    owners = lax.axis_size("fsdp")
    nt = owners // ny
    bs = left_gram.shape[2]
    stripe, width = grads.shape[2], grads.shape[3]
    jb = width // bs
    mj = 2 * jb
    cw = bs // 8
    sr = stripe // ny
    rr = stripe // 4
    vm = pltpu.VMEM
    scratch = [
        vm((2, ny, sr, width), BF16),
        vm((2, 2, 2, jb, ny, sr, cw), BF16),
        vm((2, 2, jb, ny, sr, cw), BF16),
        vm((2, 2, jb, ny, sr, cw), BF16),
        vm((2, ny, mj, sr, cw), BF16),
        vm((ny * mj, sr, cw), BF16),
        vm((ny * mj, sr, cw), BF16),
        vm((2, nt, ny, sr, cw), BF16),
        vm((4, nt, ny, sr, 2 * cw), BF16),
        vm((2, bs // 4, bs), BF16),
        vm((2, bs, 2 * cw), BF16),
        vm((bs // 2, 2 * cw), BF16),
        vm((2, bs // 2, 2 * cw), F32),
        vm((2, 2, nt // 4, 2, 4, rr, cw), BF16),
        vm((2, ny, 2, nt // 2, rr, cw), BF16),
        vm((nt * ny, rr, cw), BF16),
        vm((nt * ny, rr, cw), BF16),
        vm((2, ny, mj, rr, cw), BF16),
        vm((2, ny, mj, rr, cw), BF16),
        vm((1, 128), jnp.int32),
        pltpu.SMEM((ny * nt,), jnp.int32),
        pltpu.SMEM((ny * nt,), jnp.int32),
        pltpu.SMEM((1, 128), jnp.int32),
        pltpu.SemaphoreType.DMA((N_LOCAL,)),
        pltpu.SemaphoreType.DMA((N_SEND,)),
        pltpu.SemaphoreType.DMA((N_RECV,)),
    ]
    whole = pl.BlockSpec(memory_space=pltpu.HBM)
    inside = pl.BlockSpec(memory_space=pltpu.VMEM)
    operands = (
        slot_block, grads.reshape(2, ny, sr, width), left_gram, right_gram, left_root, right_root
    )
    outs = pl.pallas_call(
        functools.partial(kernel, (ny, nt, jb, cw)),
        out_shape=(
            pltpu.VMEM(left_gram.shape, F32),
            pltpu.VMEM(right_gram.shape, F32),
            pltpu.VMEM((2, rr, width), BF16),
        ),
        in_specs=[whole, whole, whole, whole, whole, whole],
        out_specs=(inside,) * 3,
        scratch_shapes=scratch,
        compiler_params=pltpu.CompilerParams(
            collective_id=0, has_side_effects=True, vmem_limit_bytes=48 * 1024 * 1024
        ),
        cost_estimate=pl.CostEstimate(
            flops=5 * bs**3 // 2, bytes_accessed=12 * bs * bs, transcendentals=0
        ),
        name="shampoo",
    )(
        *(pltpu.with_memory_space_constraint(a, pltpu.HBM) for a in operands)
    )
    return pl.pallas_call(
        hand_on,
        out_shape=tuple(pltpu.HBM(a.shape, a.dtype) for a in outs),
        in_specs=[inside] * 3,
        out_specs=(whole,) * 3,
        scratch_shapes=[pltpu.SemaphoreType.DMA((3,))],
        name="hand_on",
    )(*(pltpu.with_memory_space_constraint(a, pltpu.VMEM) for a in outs))


def solution(mesh, ny=4):
    in_specs = (
        P("rep", None, "fsdp", None),
        P(),
        P("fsdp", "rep", None),
        P("fsdp", "rep", None),
        P("fsdp", "rep", None),
        P("fsdp", None, "rep"),
    )
    out_specs = (P("fsdp", "rep", None), P("fsdp", "rep", None), P(None, ("fsdp", "rep"), None))
    return jax.shard_map(
        functools.partial(body, ny), mesh=mesh, in_specs=in_specs, out_specs=out_specs,
        check_vma=False,
    )
```

```python
import functools

import jax
import jax.numpy as jnp
from jax import lax
from jax.experimental import pallas as pl
from jax.experimental.pallas import tpu as pltpu
from jax.sharding import PartitionSpec as P

MESH = pl.DeviceIdType.MESH
BF16 = jnp.bfloat16
F32 = jnp.float32
N_LOCAL, N_SEND, N_RECV = 20, 64, 64


def dot(a, b, dims):
    return lax.dot_general(a, b, (dims, ((), ())), preferred_element_type=F32)


def kernel(
    sizes,
    slot_block, grads, left_gram, right_gram, left_root, right_root,
    lg, rg, upd,
    gv, rs1, psend, rs2, ysum, yrecv0, yrecv1, tsend, g, l2, r2, nbuf, total, pbuf, pa, pb0, pb1,
    csend, cr, place_row, slot_table, fetch, slot_place, lsem, ssem, rsem,
):
    ny, nt, jb, cw = sizes
    mj = 2 * jb
    bs = 8 * cw
    half = nt // 2
    per = nt // 4
    rr = bs // nt // 4
    yrecv = (yrecv0, yrecv1)
    s = lax.axis_index("fsdp")
    x = lax.axis_index("rep")
    y = lax.div(s, nt)
    t = lax.rem(s, nt)
    xa = x + 1 - 2 * lax.rem(x, 2)
    xb = 3 - x
    xo = lax.rem(x + 2, 4)
    xhalf = lax.div(x, 2)
    pair = jnp.minimum(x, xb)
    y_steps = (ny // 2, *[d for d in range(1, ny) if d != ny // 2])

    counters = {"l": 0, "s": 0, "r": 0}

    def take(kind):
        counters[kind] += 1
        return counters[kind] - 1

    sends = []
    own = {}

    def dev(xx, yy, tt):
        return (yy * nt + tt, xx)

    def remote(src, dst, si, ri, to):
        pltpu.make_async_remote_copy(
            src_ref=src, dst_ref=dst, send_sem=ssem.at[si], recv_sem=rsem.at[ri],
            device_id=to, device_id_type=MESH,
        ).start()

    def local(src, dst):
        copy = pltpu.make_async_copy(src, dst, lsem.at[take("l")])
        copy.start()
        return copy

    def await_recv(ref, ri):
        pltpu.make_async_copy(ref, ref, rsem.at[ri]).wait()

    barrier = pltpu.get_barrier_semaphore()
    for to in ((xa, y), (xb, y), *((x, lax.rem(y + d, 4)) for d in (1, 2, 3))):
        pl.semaphore_signal(barrier, inc=1, device_id=dev(*to, t), device_id_type=MESH)

    def greet(d, carry):
        to = dev(x, y, lax.rem(t + d, nt))
        pl.semaphore_signal(barrier, inc=1, device_id=to, device_id_type=MESH)
        return carry

    lax.fori_loop(1, nt, greet, 0)

    copy_table = local(slot_block, slot_table)
    copy_gv = local(grads, gv)
    copy_l = local(left_root.at[0], l2.at[lax.rem(x, 2)])
    copy_r = local(right_root.at[0], r2.at[xhalf])
    copy_lg = local(left_gram, lg)
    copy_rg = local(right_gram, rg)
    pl.semaphore_wait(barrier, 5 + nt - 1)

    def fourth(k):
        return pl.ds(pl.multiple_of(lax.rem(k, 4) * 2 * cw, 2 * cw), 2 * cw)

    def outward(k, n):
        return n // 2 + lax.div(k + 1, 2) * (1 - 2 * lax.rem(k, 2))

    def cols(j, q, c):
        return pl.ds(pl.multiple_of(j * bs + q * 2 * cw + c * cw, cw), cw)

    rs1_r = [[[take("r") for _ in range(2)] for _ in range(2)] for _ in range(2)]
    rs2_r = [[take("r") for _ in range(2)] for _ in range(2)]

    def rs1_start(c):
        for w in (1, 0):
            si = [take("s") for _ in range(2)]

            def one(j, carry, w=w, si=si):
                for m, to_x in enumerate((xa, xb)):
                    q = xo if w == 1 else to_x
                    remote(
                        grads.at[m, :, :, cols(j, q, c)], rs1.at[c, m, w, j],
                        si[m], rs1_r[c][m][w], dev(to_x, y, t),
                    )
                return carry

            lax.fori_loop(0, jb, one, 0)
            for m in range(2):
                sends.append((rs1.at[c, m, w], si[m]))

    def rs2_start(c):
        for m, to_x in enumerate((xb, xa)):
            await_recv(rs1.at[c, m, 1], rs1_r[c][m][1])

            def one(j, carry, m=m, to_x=to_x):
                mine = gv[m, :, :, cols(j, to_x, c)].astype(F32)
                psend[c, m, j] = (mine + rs1[c, m, 1, j].astype(F32)).astype(BF16)
                return carry

            lax.fori_loop(0, jb, one, 0, unroll=True)
            si = take("s")
            remote(psend.at[c, m], rs2.at[c, m], si, rs2_r[c][m], dev(to_x, y, t))
            sends.append((psend.at[c, m], si))

    y1_r = [take("r") for _ in range(2)]
    t_r = [[take("r") for _ in range(2)] for _ in range(2)]

    def y1_start(c):
        si = take("s")
        for m in range(2):
            await_recv(rs1.at[c, m, 0], rs1_r[c][m][0])
            await_recv(rs2.at[c, m], rs2_r[c][m])

            def one(j, carry, m=m):
                mine = gv[m, :, :, cols(j, x, c)].astype(F32)
                whole = mine + rs1[c, m, 0, j].astype(F32) + rs2[c, m, j].astype(F32)
                ysum[c, :, m * jb + j] = whole.astype(BF16)
                return carry

            lax.fori_loop(0, jb, one, 0, unroll=True)
            blocks = pl.ds(m * jb, jb)
            place = yrecv[c].at[pl.ds(y * mj + m * jb, jb)]
            for d in y_steps:
                yy = lax.rem(y + d, ny)
                remote(ysum.at[c, yy, blocks], place, si, y1_r[c], dev(x, yy, t))
            own["y1", c, m] = local(ysum.at[c, y, blocks], place)
        sends.append((ysum.at[c, pl.ds(0, ny - 1)], si))

    def t_bytes(c, k):
        return tsend.at[c, 0, pl.ds(0, 3)] if k else tsend.at[c, pl.ds(0, nt - 1)]

    def t_start(c):
        await_recv(yrecv[c].at[pl.ds(0, 3 * mj)], y1_r[c])
        for m in range(2):
            own["y1", c, m].wait()
        si = [take("s") for _ in range(2)]
        place = g.at[x, t, y, :, gcols(c)]

        def pick(tt, dy):
            yy = lax.rem(y + dy, 4)
            tsend[c, tt, yy] = yrecv[c][fetch[yy * nt + tt]]
            return tsend.at[c, tt, yy], dev(x, yy, tt)

        def one(k, carry):
            tt = lax.rem(t + outward(k, nt), nt)
            for dy in (2, 1, 3, 0):
                src, to = pick(tt, dy)
                remote(src, place, si[0], t_r[c][0], to)
            return carry

        lax.fori_loop(0, nt - 1, one, 0)
        for dy in (2, 1, 3):
            src, to = pick(t, dy)
            remote(src, place, si[1], t_r[c][1], to)
        src, _ = pick(t, 0)
        own["t", c] = local(src, place)
        for k in range(2):
            sends.append((t_bytes(c, k), si[k]))

    def gcols(c):
        return pl.ds(c * cw, cw)

    ag1_r = [[[take("r") for _ in range(2)] for _ in range(2)] for _ in range(2)]
    ag2_r = [[take("r") for _ in range(2)] for _ in range(2)]

    def gpart(q, h, c):
        return g.at[q, pl.ds(h * half, half), :, :, gcols(c)]

    def ag1_start(c):
        for k in range(2):
            await_recv(t_bytes(c, k), t_r[c][k])
        own["t", c].wait()
        for first in (True, False):
            for e, to_x in enumerate((xa, xb)):
                h = e if first else 1 - e
                part = gpart(x, h, c)
                si = take("s")
                remote(part, part, si, ag1_r[c][e][h], dev(to_x, y, t))
                sends.append((part, si))

    def ag2_start(c):
        for e, (source, to_x) in enumerate(((xa, xb), (xb, xa))):
            part = gpart(source, e, c)
            await_recv(part, ag1_r[c][e][e])
            si = take("s")
            remote(part, part, si, ag2_r[c][e], dev(to_x, y, t))
            sends.append((part, si))

    rs1_start(0)
    copy_table.wait()
    lanes = lax.broadcasted_iota(jnp.int32, place_row.shape, 1)

    def turn(k, row):
        b = slot_table[k]
        fetch[k] = lax.rem(lax.div(b, jb), ny) * mj + lax.div(b, jb * ny) * jb + lax.rem(b, jb)
        at = lax.rem(k, nt) * ny + lax.div(k, nt)
        return jnp.where(lanes == b, at, row)

    place_row[...] = lax.fori_loop(0, ny * nt, turn, jnp.zeros_like(lanes))
    copy_place = local(place_row, slot_place)
    copy_gv.wait()
    rs2_start(0)
    rs1_start(1)
    y1_start(0)
    rs2_start(1)
    t_start(0)
    l_s, r_s, l_r, r_r = take("s"), take("s"), take("r"), take("r")
    mine_l, mine_r = lax.rem(x, 2), xhalf
    for k in range(1, 4):
        square = fourth(xa + k)
        remote(
            left_root.at[0, :, square], l2.at[mine_l, :, square], l_s, l_r, dev(xa, y, t)
        )
        square = fourth(xb + k)
        remote(
            right_root.at[0, square], r2.at[mine_r, square], r_s, r_r, dev(xb, y, t)
        )
    l_bytes = l2.at[0, :, pl.ds(0, 6 * cw)]
    r_bytes = r2.at[0, pl.ds(0, 6 * cw)]
    sends.append((l_bytes, l_s))
    sends.append((r_bytes, r_s))
    y1_start(1)
    t_start(1)
    copy_l.wait()
    l2[1 - mine_l, :, fourth(x)] = l2[mine_l, :, fourth(xa)].T
    copy_r.wait()
    r2[1 - mine_r, fourth(x)] = r2[mine_r, fourth(xb)].T
    ag1_start(0)
    ag2_start(0)
    ag1_start(1)

    def block_cols(q):
        return g[q].reshape(bs, 2 * cw)

    def rows_times(q):
        part = dot(l2[...].reshape(bs // 2, bs), block_cols(q), ((1,), (0,)))
        return part.astype(BF16)

    def product(c, q):
        return dot(nbuf[...], r2[c, fourth(q)], ((1,), (0,)))

    await_recv(l_bytes, l_r)
    await_recv(r_bytes, r_r)
    nbuf[...] = rows_times(x)
    for c in range(2):
        total[c] = product(c, x)
    ag2_start(1)
    for e, source in enumerate((xa, xb)):
        await_recv(gpart(source, 1 - e, 0), ag1_r[0][e][1 - e])
        await_recv(gpart(source, 1 - e, 1), ag1_r[1][e][1 - e])
        nbuf[...] = rows_times(source)
        for c in range(2):
            total[c] += product(c, source)
    for c in range(2):
        for e in range(2):
            await_recv(gpart(xo, e, c), ag2_r[c][e])

    z, core = lax.div(t, 2), lax.rem(t, 2)
    quads = nt // 4
    batches = (min(2, quads), 1)
    a_s = [[[take("s") for _ in range(2)] for _ in range(n)] for n in batches]
    a_r = [[[take("r") for _ in range(2)] for _ in range(n)] for n in batches]

    def a_start(c):
        n = quads // batches[c]
        size = bs // 2 // batches[c]
        for i in range(batches[c]):
            rows = pl.ds(i * size, size)
            if c == 0:
                left = l2[...].reshape(bs // 2, bs)[i * size : (i + 1) * size]
                nbuf[rows] = dot(left, block_cols(xo), ((1,), (0,))).astype(BF16)
            last = dot(nbuf[rows], r2[c, fourth(xo)], ((1,), (0,)))
            part = (total[c, rows] + last).astype(BF16)
            for h in range(2):
                piece = part[:, h * cw : (h + 1) * cw].reshape(n, 2, 4, rr, cw)
                pbuf[c, h, pl.ds(i * n, n)] = piece
            place = pa.at[c, y, pair, pl.ds(xhalf * quads + i * n, n)]
            for dx in (2, 1, 3, 0):
                for dy in (2, 1, 3, 0):
                    xx, yy = lax.rem(x + dx, 4), lax.rem(y + dy, 4)
                    tp = lax.rem(yy + c, 2)
                    src = pbuf.at[c, lax.div(yy, 2), pl.ds(i * n, n), tp, xx]
                    k = 0 if dx else 1
                    if dx or dy:
                        remote(src, place, a_s[c][i][k], a_r[c][i][k], dev(xx, yy, t))
                    else:
                        own["a", c, i] = local(src, place)
            for k in range(2):
                sends.append((a_bytes(c, k), a_s[c][i][k]))

    def a_bytes(c, k):
        n = quads // batches[c]
        return pa.at[c, pl.ds(0, 3), 0, pl.ds(0, n)] if k else pa.at[c, pl.ds(0, 3), :, pl.ds(0, 2 * n)]

    pb = (pb0, pb1)
    b_s = [take("s") for _ in range(2)]
    b_r = [take("r") for _ in range(2)]
    b_place = pl.ds(t * 4, 4)
    b_bytes = pl.ds(0, (nt - 1) * 4)

    def b_start(c, i):
        for k in range(2):
            await_recv(a_bytes(c, k), a_r[c][i][k])
        own["a", c, i].wait()
        n = quads // batches[c]
        for p in range(2):

            def stripe(k, carry, p=p):
                if batches[c] == 1:
                    zz = lax.rem(z + outward(k, nt // 2), nt // 2)
                else:
                    j = lax.rem(k + z, 2 * n)
                    zz = lax.rem(j, 2) * quads + i * n + lax.div(j, 2)

                @pl.when(zz != z)
                def _():
                    to = dev(x, y, 2 * zz + lax.rem(y + c, 2))
                    remote(pa.at[c, :, p, zz], pb[p].at[b_place], b_s[p], b_r[p], to)

                return carry

            lax.fori_loop(0, 2 * n, stripe, 0)

    a_start(0)
    a_start(1)
    for i in range(batches[0]):
        b_start(0, i)
    copy_lg.wait()
    for q in range(4):
        rows = g[q, pl.ds(x * per, per)].reshape(bs // 4, 2 * cw)
        lg[0] += dot(rows, block_cols(q), ((1,), (1,)))
    b_start(1, 0)
    here = lax.rem(core + y, 2)
    for p in range(2):
        to = dev(x, y, 2 * z + 1 - core)
        remote(pa.at[1 - here, :, p, z], pb[p].at[b_place], b_s[p], b_r[p], to)
        own["b", p] = local(pa.at[here, :, p, z], pb[p].at[b_place])
        sends.append((pb[p].at[b_bytes], b_s[p]))

    copy_rg.wait()
    turned = block_cols(x).T
    for q in range(4):
        part = pl.ds(q * 2 * cw, 2 * cw)
        rg[0, :, part] += dot(turned, block_cols(q), ((1,), (0,)))

    copy_place.wait()

    def collect(p, yy):
        def one(j, carry):
            for m in range(2):
                csend[p, yy, m * jb + j] = pb[p][slot_place[0, (m * 4 + yy) * jb + j]]
            return carry

        lax.fori_loop(0, jb, one, 0, unroll=True)

    c_s = [[take("s") for _ in range(4)] for _ in range(2)]
    c_r = [[take("r") for _ in range(4)] for _ in range(2)]
    for p in range(2):
        await_recv(pb[p].at[b_bytes], b_r[p])
        own["b", p].wait()
        for d in y_steps:
            yy = lax.rem(y + d, 4)
            collect(p, yy)
            remote(csend.at[p, yy], cr.at[p, y], c_s[p][d], c_r[p][d], dev(x, yy, t))
            sends.append((csend.at[p, 0], c_s[p][d]))

    def lay(src, p, yy):
        quarter = p + lax.rem(core + yy, 2) * (3 - 2 * p)

        def one(j, carry):
            for m in range(2):
                at = j * bs + quarter * 2 * cw + lax.div(yy, 2) * cw
                upd[m, :, pl.ds(pl.multiple_of(at, cw), cw)] = src[p, yy, m * jb + j]
            return carry

        lax.fori_loop(0, jb, one, 0, unroll=True)

    for p in range(2):
        collect(p, y)
        lay(csend, p, y)
    for p in range(2):
        for d in y_steps:
            yy = lax.rem(y - d + 4, 4)
            await_recv(cr.at[p, yy], c_r[p][d])
            lay(cr, p, yy)

    for ref, si in sends:
        pltpu.make_async_copy(ref, ref, ssem.at[si]).wait()
    assert counters["l"] <= N_LOCAL and counters["s"] <= N_SEND and counters["r"] <= N_RECV


def hand_on(*refs):
    sem = refs[-1]
    copies = [pltpu.make_async_copy(refs[i], refs[3 + i], sem.at[i]) for i in range(3)]
    for copy in copies:
        copy.start()
    for copy in copies:
        copy.wait()


def body(ny, grads, slot_block, left_gram, right_gram, left_root, right_root):
    owners = lax.axis_size("fsdp")
    nt = owners // ny
    bs = left_gram.shape[2]
    stripe, width = grads.shape[2], grads.shape[3]
    jb = width // bs
    mj = 2 * jb
    cw = bs // 8
    sr = stripe // ny
    rr = stripe // 4
    vm = pltpu.VMEM
    scratch = [
        vm((2, ny, sr, width), BF16),
        vm((2, 2, 2, jb, ny, sr, cw), BF16),
        vm((2, 2, jb, ny, sr, cw), BF16),
        vm((2, 2, jb, ny, sr, cw), BF16),
        vm((2, ny, mj, sr, cw), BF16),
        vm((ny * mj, sr, cw), BF16),
        vm((ny * mj, sr, cw), BF16),
        vm((2, nt, ny, sr, cw), BF16),
        vm((4, nt, ny, sr, 2 * cw), BF16),
        vm((2, bs // 4, bs), BF16),
        vm((2, bs, 2 * cw), BF16),
        vm((bs // 2, 2 * cw), BF16),
        vm((2, bs // 2, 2 * cw), F32),
        vm((2, 2, nt // 4, 2, 4, rr, cw), BF16),
        vm((2, ny, 2, nt // 2, rr, cw), BF16),
        vm((nt * ny, rr, cw), BF16),
        vm((nt * ny, rr, cw), BF16),
        vm((2, ny, mj, rr, cw), BF16),
        vm((2, ny, mj, rr, cw), BF16),
        vm((1, 128), jnp.int32),
        pltpu.SMEM((ny * nt,), jnp.int32),
        pltpu.SMEM((ny * nt,), jnp.int32),
        pltpu.SMEM((1, 128), jnp.int32),
        pltpu.SemaphoreType.DMA((N_LOCAL,)),
        pltpu.SemaphoreType.DMA((N_SEND,)),
        pltpu.SemaphoreType.DMA((N_RECV,)),
    ]
    whole = pl.BlockSpec(memory_space=pltpu.HBM)
    inside = pl.BlockSpec(memory_space=pltpu.VMEM)
    operands = (
        slot_block, grads.reshape(2, ny, sr, width), left_gram, right_gram, left_root, right_root
    )
    outs = pl.pallas_call(
        functools.partial(kernel, (ny, nt, jb, cw)),
        out_shape=(
            pltpu.VMEM(left_gram.shape, F32),
            pltpu.VMEM(right_gram.shape, F32),
            pltpu.VMEM((2, rr, width), BF16),
        ),
        in_specs=[whole, whole, whole, whole, whole, whole],
        out_specs=(inside,) * 3,
        scratch_shapes=scratch,
        compiler_params=pltpu.CompilerParams(
            collective_id=0, has_side_effects=True, vmem_limit_bytes=48 * 1024 * 1024
        ),
        cost_estimate=pl.CostEstimate(
            flops=5 * bs**3 // 2, bytes_accessed=12 * bs * bs, transcendentals=0
        ),
        name="shampoo",
    )(
        *(pltpu.with_memory_space_constraint(a, pltpu.HBM) for a in operands)
    )
    return pl.pallas_call(
        hand_on,
        out_shape=tuple(pltpu.HBM(a.shape, a.dtype) for a in outs),
        in_specs=[inside] * 3,
        out_specs=(whole,) * 3,
        scratch_shapes=[pltpu.SemaphoreType.DMA((3,))],
        name="hand_on",
    )(*(pltpu.with_memory_space_constraint(a, pltpu.VMEM) for a in outs))


def solution(mesh, ny=4):
    in_specs = (
        P("rep", None, "fsdp", None),
        P(),
        P("fsdp", "rep", None),
        P("fsdp", "rep", None),
        P("fsdp", "rep", None),
        P("fsdp", None, "rep"),
    )
    out_specs = (P("fsdp", "rep", None), P("fsdp", "rep", None), P(None, ("fsdp", "rep"), None))
    return jax.shard_map(
        functools.partial(body, ny), mesh=mesh, in_specs=in_specs, out_specs=out_specs,
        check_vma=False,
    )
```
